32 devices in a mesh: groups: 2 (over x), sites: 16 (over z, y, core).
Axes of the slice: x: 2, y: 2, z: 4, core: 2. Of those that a mesh axis runs over, the one named last changes fastest.
Arguments:
- tip_probs: bfloat16 [128, 20, 8192], P(('groups', 'sites')), parts along dimension 0, may hold values from 0.02 to 600, as said below
- leaf_order: int32 [128], P('groups'), parts along dimension 0, may hold values from 0 to 63, each once
- site_weights: int32 [16384], P(('groups', 'sites')), parts along dimension 0, may hold values from 1 to 10
- branch_length: float32 [252], P('groups'), parts along dimension 0, may hold values from 0.02 to 0.6
- direction: float32 [252], P('groups'), parts along dimension 0, may hold values from -6 to 6
Outputs:
- gradient: float32 [252], P('groups'), parts along dimension 0
- hess_vec: float32 [252], P('groups'), parts along dimension 0
The draws below stay inside these ranges and needn't reach their ends.
There are 2 independent parts, one for each index of `groups`. The reference program is written for one: setup_inputs(seed, part) draws one part's arguments, and reference() takes and returns one part's arrays. A program takes and returns all parts, laid end to end along the dimension named above; each array names one. Nothing has to cross between parts.
Inputs may be any that keep to these rules, and one draw needn't show every extreme that they name: `tip_probs`: positive state likelihoods.
All inputs are finite; a program needn't handle non-finite values.
Results may differ from the reference program's by a relative error of at most 0.0003.
Values may be sent and summed in bfloat16 or wider, within the bound.
No kernel may reach another device: no remote copies, remote signals or barrier semaphores. Data moves between devices by JAX's collectives and lax.ppermute only.
A program may use at most 128 MiB of HBM per device.

```python
import math
import jax
import jax.numpy as jnp
from jax import lax

STATES = 20
TILE = 128
TIPS = 64
BRANCHES = 126
SITES = 8192


def draw_tip_probs(key, part):
    key = jax.random.fold_in(key, 11)
    call_key, jitter_key = jax.random.split(key)
    called = jax.random.randint(call_key, (TIPS, 1, SITES), 0, STATES)
    states_row = jnp.arange(STATES, dtype=jnp.int32).reshape(1, STATES, 1)
    boosted = jnp.where(states_row == called, 16.0, 1.0)
    jitter = jnp.clip(jax.random.normal(jitter_key, (TIPS, STATES, SITES), jnp.float32), -3.0, 3.0)
    return (jnp.exp(1.2 * jitter) * boosted).astype(jnp.bfloat16)


def draw_site_weights(key, part):
    key = jax.random.fold_in(key, 23)
    position = jnp.arange(SITES, dtype=jnp.int32)
    ceiling = 2 + 10 * position // SITES
    return jax.random.randint(key, (SITES,), 1, ceiling).astype(jnp.int32)


def normal_values(own_key, shape, scale, reach, held_as=jnp.bfloat16):
    values = scale * jax.random.normal(own_key, shape, jnp.float32)
    return jnp.clip(values, min=-reach, max=reach).astype(held_as)


def setup_inputs(seed: int = 0, part: int = 0) -> dict:
    arg_keys = jax.random.split(jax.random.key(seed), 6)
    part_splits = jax.random.split(jax.random.fold_in(arg_keys[5], part), 6)
    return {
        "tip_probs": draw_tip_probs(jax.random.fold_in(jax.random.fold_in(arg_keys[5], part), 71), part),
        "leaf_order": jax.random.permutation(part_splits[1], TIPS).astype(jnp.int32),
        "site_weights": draw_site_weights(jax.random.fold_in(jax.random.fold_in(arg_keys[5], part), 71), part),
        "branch_length": jnp.clip(jnp.exp(jax.random.uniform(part_splits[3], (BRANCHES,), jnp.float32, math.log(0.02), math.log(0.6))), 0.02, 0.6),
        "direction": normal_values(part_splits[4], (BRANCHES,), 1.0, 6.0, jnp.float32),
    }


def site_loglik(lengths, leaves, leaf_order):
    tip_count = leaves.shape[0]
    decay_rate = leaves.shape[1] / (leaves.shape[1] - 1.0)
    slot_match = leaf_order[:, None] == lax.broadcasted_iota(jnp.int32, (tip_count, tip_count), 1)
    branch = jnp.dot(slot_match.astype(lengths.dtype), lengths[:tip_count], precision=lax.Precision.HIGHEST)
    inside = leaves
    log_scale = jnp.zeros(leaves.shape[2:], leaves.dtype)
    offset = tip_count
    level_size = tip_count
    while level_size > 1:
        stay_prob = jnp.exp(-decay_rate * branch)[:, None, :]
        carried = stay_prob * inside + (1.0 - stay_prob) * lax.optimization_barrier(jnp.mean(inside, axis=1, keepdims=True))
        paired = carried.reshape(level_size // 2, 2, carried.shape[1], carried.shape[2])
        joined = paired[:, 0] * paired[:, 1]
        node_sum = lax.optimization_barrier(jnp.sum(joined, axis=1))
        inside = joined / node_sum[:, None, :]
        log_scale = log_scale + lax.optimization_barrier(jnp.sum(jnp.log(node_sum), axis=0))
        level_size = level_size // 2
        branch = lengths[offset:offset + level_size]
        offset = offset + level_size
    return jnp.sum(jnp.log(lax.optimization_barrier(jnp.mean(inside[0], axis=0))) + log_scale)

def site_terms(tile_data, leaf_order, branch_length, direction):
    leaves = jnp.take(tile_data, leaf_order, axis=0).astype(jnp.float32)
    site_count = leaves.shape[2]
    lengths = jnp.broadcast_to(branch_length[:, None], (branch_length.shape[0], site_count))
    toward = jnp.broadcast_to(direction[:, None], lengths.shape)

    def loglik(spread):
        return site_loglik(spread, leaves, leaf_order)
    return jax.jvp(jax.grad(loglik), (lengths,), (toward,))

def reference(tip_probs, leaf_order, site_weights, branch_length, direction):
    tile_count = SITES // TILE
    weights = site_weights.astype(branch_length.dtype).reshape(tile_count, TILE)

    def accumulate(running, number):
        tile_data = lax.dynamic_slice_in_dim(tip_probs, number * TILE, TILE, 2)
        site_grad, site_curve = site_terms(tile_data, leaf_order, branch_length, direction)
        weight = lax.dynamic_index_in_dim(weights, number, 0, keepdims=False)
        return ((running[0] + lax.optimization_barrier(jnp.sum(site_grad * weight, axis=1)), running[1] + lax.optimization_barrier(jnp.sum(site_curve * weight, axis=1))), None)
    zeroed = jnp.zeros_like(branch_length)
    (gradient, curvature), unused = lax.scan(accumulate, (zeroed, zeroed), jnp.arange(tile_count, dtype=jnp.int32))
    weight_total = jnp.sum(weights)
    return (gradient / weight_total, curvature / weight_total)
```

```python
import functools
import jax
import jax.numpy as jnp
from jax import lax
from jax.experimental import pallas as pl
from jax.experimental.pallas import tpu as pltpu
from jax.sharding import PartitionSpec as P

F32 = jnp.float32
LANES = 128
ROWS = 8


def deal_kernel(tips_ref, out_ref, wide_ref):
    states, tips, span = tips_ref.shape
    per_row = span // LANES
    rows = states * per_row
    for state in range(states):
        for part in range(per_row):
            wide_ref[pl.ds(state * per_row + part, tips, rows), :] = tips_ref[
                state, :, part * LANES : (part + 1) * LANES
            ].astype(F32)
    out_ref[0] = wide_ref[...].astype(out_ref.dtype)


def deal(tip_probs, peers):
    states, tips, sites = tip_probs.shape
    span = sites // peers
    rows = states * span // LANES
    return pl.pallas_call(
        deal_kernel,
        grid=(peers,),
        in_specs=[pl.BlockSpec((states, tips, span), lambda i: (0, 0, i))],
        out_specs=pl.BlockSpec((1, tips * rows, LANES), lambda i: (i, 0, 0)),
        out_shape=jax.ShapeDtypeStruct((peers, tips * rows, LANES), tip_probs.dtype),
        scratch_shapes=[pltpu.VMEM((tips * rows, LANES), F32)],
        name="deal_tips",
    )(tip_probs)


def part_sum(x):
    return jnp.sum(x, axis=0)


def both(half):
    return half + pltpu.roll(half, half.shape[0] // 2, 0)


def prune_kernel(
    order_ref, x_ref, weight_ref, length_ref, toward_ref, out_ref,
    rate_ref, slope_ref, sums_ref, dsums_ref, y_ref, dy_ref, adj_ref, dadj_ref, norm_ref, grad_ref, curve_ref,
    *, tips, states,
):
    blocks = states * 4 // ROWS
    decay = states / (states - 1.0)
    branches = length_ref.shape[1]
    length = length_ref[...]
    toward = toward_ref[...]
    grow = jnp.exp(decay * length)
    pad = LANES - branches

    def column(row):
        wide = jnp.concatenate([row, jnp.zeros((1, pad), F32)], axis=1)
        return jnp.transpose(jnp.broadcast_to(wide, (LANES, LANES)))

    rate_ref[...] = column((grow - 1.0) / states)
    slope_ref[...] = column(decay * toward * grow / states)
    grad_ref[...] = jnp.zeros_like(grad_ref)
    curve_ref[...] = jnp.zeros_like(curve_ref)
    raw = weight_ref[...].astype(F32)
    quarter = [raw[:, part * LANES : (part + 1) * LANES] for part in range(4)]
    weight = jnp.concatenate(quarter + quarter, axis=0)

    offsets = [0]
    size = tips
    while size > 1:
        offsets.append(offsets[-1] + size)
        size //= 2

    def row(ref, at):
        return jnp.broadcast_to(ref[pl.ds(at, 1), :], (ROWS, LANES))

    def leaf(slot):
        tip = order_ref[slot]
        x = x_ref[tip].astype(F32).reshape(blocks, ROWS, LANES)
        total = both(part_sum(x))
        lift = row(rate_ref, tip) * total
        y = x + lift[None]
        y_ref[slot] = y
        sums_ref[slot] = total
        return y, row(slope_ref, tip) * total, total + states * lift

    def cherry(k):
        ya, qa, ta = leaf(2 * k)
        yb, qb, tb = leaf(2 * k + 1)
        z = ya * yb
        dz = qa[None] * yb + qb[None] * ya
        return z, dz, both(part_sum(z)), qa * tb + qb * ta

    def inner(at, z, dz, total, dtotal):
        rate, slope = row(rate_ref, at), row(slope_ref, at)
        y = z + (rate * total)[None]
        dy = dz + (rate * dtotal + slope * total)[None]
        y_ref[at] = y
        dy_ref[at - tips] = dy
        sums_ref[at] = total
        dsums_ref[at - tips] = dtotal
        return y, dy

    def join(left, right):
        (ya, dya), (yb, dyb) = left, right
        z = ya * yb
        dz = dya * yb + ya * dyb
        return z, dz, both(part_sum(z)), both(part_sum(dz))

    def climb(level, k, low):
        if level == 1:
            return cherry(k)
        kids = []
        for child in (2 * k, 2 * k + 1):
            kids.append(inner(offsets[level - 1] + child, *climb(level - 1, child, low)))
        return join(*kids)

    levels = len(offsets) - 1
    cut = 3

    def up(k, carry):
        z, dz, total, dtotal = climb(cut, k, 0)
        scale = states / total
        norm_ref[k] = scale
        inner(offsets[cut] + k, z * scale[None], dz * scale[None], jnp.full_like(total, states), dtotal * scale)
        return carry

    lax.fori_loop(0, tips >> cut, up, 0)

    def fetch(at):
        return y_ref[at], dy_ref[at - tips]

    def climb_top(level, k):
        if level == cut:
            return fetch(offsets[cut] + k)
        kids = [climb_top(level - 1, 2 * k), climb_top(level - 1, 2 * k + 1)]
        raw_values = join(*kids)
        if level == levels:
            return raw_values
        return inner(offsets[level] + k, *raw_values)

    _, _, total, dtotal = climb_top(levels, 0)
    seed = 1.0 / total
    dseed = -(dtotal * seed) * seed

    def record(at, grad, curve):
        grad_ref[pl.ds(at, 1), :] = jnp.sum(weight * grad, axis=0, keepdims=True)
        curve_ref[pl.ds(at, 1), :] = jnp.sum(weight * curve, axis=0, keepdims=True)

    def down(at, ybar, dybar):
        half, dhalf = part_sum(ybar), part_sum(dybar)
        total, dtotal = sums_ref[at], dsums_ref[at - tips]
        record(at, total * half, dtotal * half + total * dhalf)
        full, dfull = both(half), both(dhalf)
        rate, slope = row(rate_ref, at), row(slope_ref, at)
        xbar = ybar + (rate * full)[None]
        dxbar = dybar + (rate * dfull + slope * full)[None]
        return xbar, dxbar, full * (1.0 + states * rate)

    def split(level, k, zbar, dzbar, zsum, low, emit):
        first, second = 2 * k, 2 * k + 1
        for child, other in ((first, second), (second, first)):
            if level == 1:
                yb = y_ref[other]
                half, dhalf = part_sum(zbar * yb), part_sum(dzbar * yb)
                tip, mate = order_ref[child], order_ref[other]
                total = sums_ref[child]
                push = row(slope_ref, mate) * sums_ref[other]
                record(tip, total * half, total * (dhalf + 0.5 * (push * zsum)))
                continue
            at, mate = offsets[level - 1] + child, offsets[level - 1] + other
            yb, dyb = fetch(mate)
            xbar, dxbar, xsum = down(at, zbar * yb, dzbar * yb + zbar * dyb)
            if level - 1 == low:
                emit(child, xbar, dxbar)
            else:
                split(level - 1, child, xbar, dxbar, xsum, low, emit)

    def keep(k, xbar, dxbar):
        scale = norm_ref[k][None]
        adj_ref[k] = xbar * scale
        dadj_ref[k] = dxbar * scale

    wide = (blocks, ROWS, LANES)
    split(levels, 0, jnp.broadcast_to(seed[None], wide), jnp.broadcast_to(dseed[None], wide), None, cut, keep)

    def descend(k, carry):
        split(cut, k, adj_ref[k], dadj_ref[k], None, 0, None)
        return carry

    lax.fori_loop(0, tips >> cut, descend, 0)

    scale = decay * grow / states
    grad = jnp.sum(jnp.transpose(grad_ref[...]), axis=0, keepdims=True)[:, :branches] * scale
    curve = jnp.sum(jnp.transpose(curve_ref[...]), axis=0, keepdims=True)[:, :branches] * scale
    curve = curve + decay * toward * grad
    out_ref[...] = jnp.zeros_like(out_ref)
    out_ref[0:1, :branches] = grad
    out_ref[1:2, :branches] = curve
    out_ref[2:3, :] = jnp.broadcast_to(jnp.sum(0.5 * weight), (1, LANES))


def prune(arrived, leaf_order, site_weights, branch_length, direction):
    tips, rows, _ = arrived.shape
    states = rows // 4
    blocks = rows // ROWS
    branches = branch_length.shape[0]
    tops = branches - tips
    cut = tips >> 3
    vm = pl.BlockSpec(memory_space=pltpu.VMEM)
    vec = (blocks, ROWS, LANES)
    return pl.pallas_call(
        functools.partial(prune_kernel, tips=tips, states=states),
        in_specs=[pl.BlockSpec(memory_space=pltpu.SMEM), vm, vm, vm, vm],
        out_specs=vm,
        out_shape=jax.ShapeDtypeStruct((ROWS, LANES), F32),
        scratch_shapes=[
            pltpu.VMEM((LANES, LANES), F32),
            pltpu.VMEM((LANES, LANES), F32),
            pltpu.VMEM((branches, ROWS, LANES), F32),
            pltpu.VMEM((tops, ROWS, LANES), F32),
            pltpu.VMEM((branches, *vec), F32),
            pltpu.VMEM((tops, *vec), F32),
            pltpu.VMEM((cut, *vec), F32),
            pltpu.VMEM((cut, *vec), F32),
            pltpu.VMEM((cut, ROWS, LANES), F32),
            pltpu.VMEM((LANES, LANES), F32),
            pltpu.VMEM((LANES, LANES), F32),
        ],
        compiler_params=pltpu.CompilerParams(vmem_limit_bytes=32 * 1024 * 1024),
        name="prune",
    )(leaf_order, arrived, site_weights.reshape(1, -1), branch_length.reshape(1, -1), direction.reshape(1, -1))


def exchange(blocks):
    return lax.all_to_all(blocks, "sites", 0, 0, tiled=True)


def total_over_sites(part):
    peers = lax.axis_size("sites")
    step = 1
    while step < peers:
        part = part + lax.ppermute(part, "sites", [(i, i ^ step) for i in range(peers)])
        step *= 2
    return part


def local(tip_probs, leaf_order, site_weights, branch_length, direction):
    peers = lax.axis_size("sites")
    branches = branch_length.shape[0]
    states = tip_probs.shape[1]
    arrived = exchange(deal(jnp.transpose(tip_probs, (1, 0, 2)), peers))
    arrived = arrived.reshape(leaf_order.shape[0], -1, LANES)
    sums = total_over_sites(prune(arrived, leaf_order, site_weights, branch_length, direction))
    weight_total = sums[2, 0]
    gradient = sums[0, :branches] / weight_total - states / (states - 1.0)
    return gradient, sums[1, :branches] / weight_total


def solution(mesh):
    return jax.shard_map(
        local,
        mesh=mesh,
        in_specs=(
            P(("groups", "sites"), None, None),
            P("groups"),
            P(("groups", "sites")),
            P("groups"),
            P("groups"),
        ),
        out_specs=(P("groups"), P("groups")),
        check_vma=False,
    )
```

```python
import functools
import jax
import jax.numpy as jnp
from jax import lax
from jax.experimental import pallas as pl
from jax.experimental.pallas import tpu as pltpu
from jax.sharding import PartitionSpec as P

F32 = jnp.float32
LANES = 128
ROWS = 8


def part_sum(x):
    return jnp.sum(x, axis=0)


def both(half):
    return half + pltpu.roll(half, half.shape[0] // 2, 0)


def prune_kernel(
    order_ref, me_ref, *refs, unpack, held, tips, states, each
):
    (weight_ref, length_ref, toward_ref), piece_refs = refs[:3], refs[3 : 3 + held]
    out_ref, wide_ref, *refs = refs[3 + held :]
    (
        rate_ref, slope_ref, sums_ref, dsums_ref, y_ref, dy_ref, adj_ref, dadj_ref, norm_ref, grad_ref, curve_ref,
    ) = refs
    rows = states * 4
    me = me_ref[0]
    unpack(piece_refs, wide_ref, me, each * rows)
    blocks = states * 4 // ROWS
    decay = states / (states - 1.0)
    branches = length_ref.shape[1]
    length = length_ref[...]
    toward = toward_ref[...]
    grow = jnp.exp(decay * length)
    pad = LANES - branches

    def column(row):
        wide = jnp.concatenate([row, jnp.zeros((1, pad), F32)], axis=1)
        return jnp.transpose(jnp.broadcast_to(wide, (LANES, LANES)))

    rate_ref[...] = column((grow - 1.0) / states)
    slope_ref[...] = column(decay * toward * grow / states)
    grad_ref[...] = jnp.zeros_like(grad_ref)
    curve_ref[...] = jnp.zeros_like(curve_ref)
    raw = weight_ref[...].astype(F32)
    quarter = [raw[:, part * LANES : (part + 1) * LANES] for part in range(4)]
    weight = jnp.concatenate(quarter + quarter, axis=0)

    offsets = [0]
    size = tips
    while size > 1:
        offsets.append(offsets[-1] + size)
        size //= 2

    def row(ref, at):
        return jnp.broadcast_to(ref[pl.ds(at, 1), :], (ROWS, LANES))

    def leaf(slot):
        tip = order_ref[slot]
        first = ((tip // each) ^ me) * (each * rows) + tip % each
        x = wide_ref[pl.ds(first, rows, each), :].reshape(blocks, ROWS, LANES)
        total = both(part_sum(x))
        lift = row(rate_ref, tip) * total
        y = x + lift[None]
        y_ref[slot] = y
        sums_ref[slot] = total
        return y, row(slope_ref, tip) * total, total + states * lift

    def cherry(k):
        ya, qa, ta = leaf(2 * k)
        yb, qb, tb = leaf(2 * k + 1)
        z = ya * yb
        dz = qa[None] * yb + qb[None] * ya
        return z, dz, both(part_sum(z)), qa * tb + qb * ta

    def inner(at, z, dz, total, dtotal):
        rate, slope = row(rate_ref, at), row(slope_ref, at)
        y = z + (rate * total)[None]
        dy = dz + (rate * dtotal + slope * total)[None]
        y_ref[at] = y
        dy_ref[at - tips] = dy
        sums_ref[at] = total
        dsums_ref[at - tips] = dtotal
        return y, dy

    def join(left, right):
        (ya, dya), (yb, dyb) = left, right
        z = ya * yb
        dz = dya * yb + ya * dyb
        return z, dz, both(part_sum(z)), both(part_sum(dz))

    def climb(level, k, low):
        if level == 1:
            return cherry(k)
        kids = []
        for child in (2 * k, 2 * k + 1):
            kids.append(inner(offsets[level - 1] + child, *climb(level - 1, child, low)))
        return join(*kids)

    levels = len(offsets) - 1
    cut = 3

    def up(k, carry):
        z, dz, total, dtotal = climb(cut, k, 0)
        scale = states / total
        norm_ref[k] = scale
        inner(offsets[cut] + k, z * scale[None], dz * scale[None], jnp.full_like(total, states), dtotal * scale)
        return carry

    lax.fori_loop(0, tips >> cut, up, 0)

    def fetch(at):
        return y_ref[at], dy_ref[at - tips]

    def climb_top(level, k):
        if level == cut:
            return fetch(offsets[cut] + k)
        kids = [climb_top(level - 1, 2 * k), climb_top(level - 1, 2 * k + 1)]
        raw_values = join(*kids)
        if level == levels:
            return raw_values
        return inner(offsets[level] + k, *raw_values)

    _, _, total, dtotal = climb_top(levels, 0)
    seed = 1.0 / total
    dseed = -(dtotal * seed) * seed

    def record(at, grad, curve):
        grad_ref[pl.ds(at, 1), :] = jnp.sum(weight * grad, axis=0, keepdims=True)
        curve_ref[pl.ds(at, 1), :] = jnp.sum(weight * curve, axis=0, keepdims=True)

    def down(at, ybar, dybar):
        half, dhalf = part_sum(ybar), part_sum(dybar)
        total, dtotal = sums_ref[at], dsums_ref[at - tips]
        record(at, total * half, dtotal * half + total * dhalf)
        full, dfull = both(half), both(dhalf)
        rate, slope = row(rate_ref, at), row(slope_ref, at)
        xbar = ybar + (rate * full)[None]
        dxbar = dybar + (rate * dfull + slope * full)[None]
        return xbar, dxbar, full * (1.0 + states * rate)

    def split(level, k, zbar, dzbar, zsum, low, emit):
        first, second = 2 * k, 2 * k + 1
        for child, other in ((first, second), (second, first)):
            if level == 1:
                yb = y_ref[other]
                half, dhalf = part_sum(zbar * yb), part_sum(dzbar * yb)
                tip, mate = order_ref[child], order_ref[other]
                total = sums_ref[child]
                push = row(slope_ref, mate) * sums_ref[other]
                record(tip, total * half, total * (dhalf + 0.5 * (push * zsum)))
                continue
            at, mate = offsets[level - 1] + child, offsets[level - 1] + other
            yb, dyb = fetch(mate)
            xbar, dxbar, xsum = down(at, zbar * yb, dzbar * yb + zbar * dyb)
            if level - 1 == low:
                emit(child, xbar, dxbar)
            else:
                split(level - 1, child, xbar, dxbar, xsum, low, emit)

    def keep(k, xbar, dxbar):
        scale = norm_ref[k][None]
        adj_ref[k] = xbar * scale
        dadj_ref[k] = dxbar * scale

    wide = (blocks, ROWS, LANES)
    split(levels, 0, jnp.broadcast_to(seed[None], wide), jnp.broadcast_to(dseed[None], wide), None, cut, keep)

    def descend(k, carry):
        split(cut, k, adj_ref[k], dadj_ref[k], None, 0, None)
        return carry

    lax.fori_loop(0, tips >> cut, descend, 0)

    scale = decay * grow / states
    grad = jnp.sum(jnp.transpose(grad_ref[...]), axis=0, keepdims=True)[:, :branches] * scale
    curve = jnp.sum(jnp.transpose(curve_ref[...]), axis=0, keepdims=True)[:, :branches] * scale
    curve = curve + decay * toward * grad
    out_ref[...] = jnp.zeros_like(out_ref)
    out_ref[0:1, :branches] = grad
    out_ref[1:2, :branches] = curve
    out_ref[2:3, :] = jnp.broadcast_to(jnp.sum(0.5 * weight), (1, LANES))


def prune(pieces, me, unpack, leaf_order, site_weights, branch_length, direction, states, each):
    tips = leaf_order.shape[0]
    blocks = states * 4 // ROWS
    branches = branch_length.shape[0]
    tops = branches - tips
    cut = tips >> 3
    vm = pl.BlockSpec(memory_space=pltpu.VMEM)
    sm = pl.BlockSpec(memory_space=pltpu.SMEM)
    vec = (blocks, ROWS, LANES)
    return pl.pallas_call(
        functools.partial(
            prune_kernel, unpack=unpack, held=len(pieces), tips=tips, states=states, each=each
        ),
        in_specs=[sm, sm] + [vm] * (3 + len(pieces)),
        out_specs=vm,
        out_shape=jax.ShapeDtypeStruct((ROWS, LANES), F32),
        scratch_shapes=[
            pltpu.VMEM((tips * states * 4, LANES), F32),
            pltpu.VMEM((LANES, LANES), F32),
            pltpu.VMEM((LANES, LANES), F32),
            pltpu.VMEM((branches, ROWS, LANES), F32),
            pltpu.VMEM((tops, ROWS, LANES), F32),
            pltpu.VMEM((branches, *vec), F32),
            pltpu.VMEM((tops, *vec), F32),
            pltpu.VMEM((cut, *vec), F32),
            pltpu.VMEM((cut, *vec), F32),
            pltpu.VMEM((cut, ROWS, LANES), F32),
            pltpu.VMEM((LANES, LANES), F32),
            pltpu.VMEM((LANES, LANES), F32),
        ],
        compiler_params=pltpu.CompilerParams(vmem_limit_bytes=32 * 1024 * 1024),
        name="prune",
    )(
        leaf_order,
        me.reshape(1),
        site_weights.reshape(1, -1),
        branch_length.reshape(1, -1),
        direction.reshape(1, -1),
        *pieces,
    )


def unpack_plain(piece_refs, wide_ref, me, rows):
    (pieces,) = piece_refs
    for number in range(pieces.shape[0]):
        wide_ref[number * rows : (number + 1) * rows, :] = pieces[number].astype(F32)


def unpack_pairs(piece_refs, wide_ref, me, rows):
    own, *got, take = piece_refs
    deep = own.shape[1]
    here = pl.ds(pl.multiple_of(lax.rem(me, 2) * deep, deep), deep)

    def put(number, block):
        wide_ref[number * rows : (number + 1) * rows, :] = block.astype(F32).reshape(rows, LANES)

    put(0, own[...])
    for apart, block in enumerate(got, 1):
        put(2 * apart, block[:, here, :])
    for apart in range(len(got) + 1):
        put(2 * apart + 1, take[apart])


def by_tile(tip_probs):
    tips, states, sites = tip_probs.shape
    tiles = sites // LANES
    shaped = tip_probs.transpose(1, 0, 2).reshape(states, tips, tiles, LANES)
    return shaped.transpose(0, 2, 1, 3).reshape(states, tiles * tips, LANES)


def exchange_plain(probs):
    peers = lax.axis_size("sites")
    states, rows, _ = probs.shape
    blocks = probs.reshape(states, peers, rows // peers, LANES).transpose(1, 0, 2, 3)
    arrived = lax.all_to_all(blocks, "sites", 0, 0, tiled=True)
    return [arrived.reshape(peers, -1, LANES)]


def exchange_pairs(probs):
    peers = lax.axis_size("sites")
    me = lax.axis_index("sites")
    chips, chip, core = peers // 2, me // 2, me % 2
    states, rows, _ = probs.shape
    deep = rows // peers

    def cut(block, first, count):
        return lax.dynamic_slice(block, (0, first, 0), (states, count, LANES))

    far_first = list(range(chips // 2, chips)) + list(range(1, chips // 2))
    got = {}
    for apart in far_first:
        swap = [(i, i ^ (2 * apart)) for i in range(peers)]
        got[apart] = lax.ppermute(cut(probs, 2 * deep * (chip ^ apart), 2 * deep), "sites", swap)
    give = [cut(probs, deep * (me ^ 1), deep)]
    give += [cut(got[apart], deep * (1 - core), deep) for apart in range(1, chips)]
    take = lax.ppermute(jnp.stack(give), "sites", [(i, i ^ 1) for i in range(peers)])
    return [cut(probs, deep * me, deep), *(got[apart] for apart in range(1, chips)), take]


def total_over_sites(part):
    peers = lax.axis_size("sites")
    step = 1
    while step < peers:
        part = part + lax.ppermute(part, "sites", [(i, i ^ step) for i in range(peers)])
        step *= 2
    return part


def local(tip_probs, leaf_order, site_weights, branch_length, direction):
    branches = branch_length.shape[0]
    each, states, _ = tip_probs.shape
    probs = by_tile(tip_probs)
    if 4 * each % 16 == 0:
        me = lax.axis_index("sites").astype(jnp.int32)
        pieces, unpack = exchange_pairs(probs), unpack_pairs
    else:
        me = jnp.zeros((), jnp.int32)
        pieces, unpack = exchange_plain(probs), unpack_plain
    part = prune(pieces, me, unpack, leaf_order, site_weights, branch_length, direction, states, each)
    sums = total_over_sites(part)[:, :branches]
    return sums[0] / sums[2] - states / (states - 1.0), sums[1] / sums[2]


def solution(mesh):
    return jax.shard_map(
        local,
        mesh=mesh,
        in_specs=(
            P(("groups", "sites"), None, None),
            P("groups"),
            P(("groups", "sites")),
            P("groups"),
            P("groups"),
        ),
        out_specs=(P("groups"), P("groups")),
        check_vma=False,
    )
```

```python
import functools
import jax
import jax.numpy as jnp
from jax import lax
from jax.experimental import pallas as pl
from jax.experimental.pallas import tpu as pltpu
from jax.sharding import PartitionSpec as P

F32 = jnp.float32
LANES = 128
ROWS = 8


def part_sum(x):
    return jnp.sum(x, axis=0)


def both(half):
    return half + pltpu.roll(half, half.shape[0] // 2, 0)


def prune_kernel(
    order_ref, me_ref, *refs, unpack, held, tips, states, each
):
    (weight_ref, length_ref, toward_ref), piece_refs = refs[:3], refs[3 : 3 + held]
    out_ref, wide_ref, *refs = refs[3 + held :]
    (
        rate_ref, slope_ref, sums_ref, dsums_ref, y_ref, dy_ref, adj_ref, dadj_ref, norm_ref, grad_ref, curve_ref,
    ) = refs
    rows = states * 4
    me = me_ref[0]
    unpack(piece_refs, wide_ref, me, each * rows)
    blocks = states * 4 // ROWS
    decay = states / (states - 1.0)
    branches = length_ref.shape[1]
    length = length_ref[...]
    toward = toward_ref[...]
    grow = jnp.exp(decay * length)
    pad = LANES - branches

    def column(row):
        wide = jnp.concatenate([row, jnp.zeros((1, pad), F32)], axis=1)
        return jnp.transpose(jnp.broadcast_to(wide, (LANES, LANES)))

    rate_ref[...] = column((grow - 1.0) / states)
    slope_ref[...] = column(decay * toward * grow / states)
    grad_ref[...] = jnp.zeros_like(grad_ref)
    curve_ref[...] = jnp.zeros_like(curve_ref)
    raw = weight_ref[...].astype(F32)
    quarter = [raw[:, part * LANES : (part + 1) * LANES] for part in range(4)]
    weight = jnp.concatenate(quarter + quarter, axis=0)

    offsets = [0]
    size = tips
    while size > 1:
        offsets.append(offsets[-1] + size)
        size //= 2

    def row(ref, at):
        return jnp.broadcast_to(ref[pl.ds(at, 1), :], (ROWS, LANES))

    def leaf(slot):
        tip = order_ref[slot]
        first = ((tip // each) ^ me) * (each * rows) + tip % each
        x = wide_ref[pl.ds(first, rows, each), :].reshape(blocks, ROWS, LANES)
        total = both(part_sum(x))
        lift = row(rate_ref, tip) * total
        y = x + lift[None]
        y_ref[slot] = y
        sums_ref[slot] = total
        return y, row(slope_ref, tip) * total, total + states * lift

    def cherry(k):
        ya, qa, ta = leaf(2 * k)
        yb, qb, tb = leaf(2 * k + 1)
        z = ya * yb
        dz = qa[None] * yb + qb[None] * ya
        return z, dz, both(part_sum(z)), qa * tb + qb * ta

    def inner(at, z, dz, total, dtotal):
        rate, slope = row(rate_ref, at), row(slope_ref, at)
        y = z + (rate * total)[None]
        dy = dz + (rate * dtotal + slope * total)[None]
        y_ref[at] = y
        dy_ref[at - tips] = dy
        sums_ref[at] = total
        dsums_ref[at - tips] = dtotal
        return y, dy

    def join(left, right):
        (ya, dya), (yb, dyb) = left, right
        z = ya * yb
        dz = dya * yb + ya * dyb
        return z, dz, both(part_sum(z)), both(part_sum(dz))

    def climb(level, k, low):
        if level == 1:
            return cherry(k)
        kids = []
        for child in (2 * k, 2 * k + 1):
            kids.append(inner(offsets[level - 1] + child, *climb(level - 1, child, low)))
        return join(*kids)

    levels = len(offsets) - 1
    cut = 3

    def up(k, carry):
        z, dz, total, dtotal = climb(cut, k, 0)
        scale = states / total
        norm_ref[k] = scale
        inner(offsets[cut] + k, z * scale[None], dz * scale[None], jnp.full_like(total, states), dtotal * scale)
        return carry

    lax.fori_loop(0, tips >> cut, up, 0)

    def fetch(at):
        return y_ref[at], dy_ref[at - tips]

    def climb_top(level, k):
        if level == cut:
            return fetch(offsets[cut] + k)
        kids = [climb_top(level - 1, 2 * k), climb_top(level - 1, 2 * k + 1)]
        raw_values = join(*kids)
        if level == levels:
            return raw_values
        return inner(offsets[level] + k, *raw_values)

    _, _, total, dtotal = climb_top(levels, 0)
    seed = 1.0 / total
    dseed = -(dtotal * seed) * seed

    def record(at, grad, curve):
        grad_ref[pl.ds(at, 1), :] = jnp.sum(weight * grad, axis=0, keepdims=True)
        curve_ref[pl.ds(at, 1), :] = jnp.sum(weight * curve, axis=0, keepdims=True)

    def down(at, ybar, dybar):
        half, dhalf = part_sum(ybar), part_sum(dybar)
        total, dtotal = sums_ref[at], dsums_ref[at - tips]
        record(at, total * half, dtotal * half + total * dhalf)
        full, dfull = both(half), both(dhalf)
        rate, slope = row(rate_ref, at), row(slope_ref, at)
        xbar = ybar + (rate * full)[None]
        dxbar = dybar + (rate * dfull + slope * full)[None]
        return xbar, dxbar, full * (1.0 + states * rate)

    def split(level, k, zbar, dzbar, zsum, low, emit):
        first, second = 2 * k, 2 * k + 1
        for child, other in ((first, second), (second, first)):
            if level == 1:
                yb = y_ref[other]
                half, dhalf = part_sum(zbar * yb), part_sum(dzbar * yb)
                tip, mate = order_ref[child], order_ref[other]
                total = sums_ref[child]
                push = row(slope_ref, mate) * sums_ref[other]
                record(tip, total * half, total * (dhalf + 0.5 * (push * zsum)))
                continue
            at, mate = offsets[level - 1] + child, offsets[level - 1] + other
            yb, dyb = fetch(mate)
            xbar, dxbar, xsum = down(at, zbar * yb, dzbar * yb + zbar * dyb)
            if level - 1 == low:
                emit(child, xbar, dxbar)
            else:
                split(level - 1, child, xbar, dxbar, xsum, low, emit)

    def keep(k, xbar, dxbar):
        scale = norm_ref[k][None]
        adj_ref[k] = xbar * scale
        dadj_ref[k] = dxbar * scale

    wide = (blocks, ROWS, LANES)
    split(levels, 0, jnp.broadcast_to(seed[None], wide), jnp.broadcast_to(dseed[None], wide), None, cut, keep)

    def descend(k, carry):
        split(cut, k, adj_ref[k], dadj_ref[k], None, 0, None)
        return carry

    lax.fori_loop(0, tips >> cut, descend, 0)

    scale = decay * grow / states
    grad = jnp.sum(jnp.transpose(grad_ref[...]), axis=0, keepdims=True)[:, :branches] * scale
    curve = jnp.sum(jnp.transpose(curve_ref[...]), axis=0, keepdims=True)[:, :branches] * scale
    curve = curve + decay * toward * grad
    out_ref[...] = jnp.zeros_like(out_ref)
    out_ref[0:1, :branches] = grad
    out_ref[1:2, :branches] = curve
    out_ref[2:3, :] = jnp.broadcast_to(jnp.sum(0.5 * weight), (1, LANES))


def prune(pieces, me, unpack, leaf_order, site_weights, branch_length, direction, states, each):
    tips = leaf_order.shape[0]
    blocks = states * 4 // ROWS
    branches = branch_length.shape[0]
    tops = branches - tips
    cut = tips >> 3
    vm = pl.BlockSpec(memory_space=pltpu.VMEM)
    sm = pl.BlockSpec(memory_space=pltpu.SMEM)
    vec = (blocks, ROWS, LANES)
    return pl.pallas_call(
        functools.partial(
            prune_kernel, unpack=unpack, held=len(pieces), tips=tips, states=states, each=each
        ),
        in_specs=[sm, sm] + [vm] * (3 + len(pieces)),
        out_specs=vm,
        out_shape=jax.ShapeDtypeStruct((ROWS, LANES), F32),
        scratch_shapes=[
            pltpu.VMEM((tips * states * 4, LANES), F32),
            pltpu.VMEM((LANES, LANES), F32),
            pltpu.VMEM((LANES, LANES), F32),
            pltpu.VMEM((branches, ROWS, LANES), F32),
            pltpu.VMEM((tops, ROWS, LANES), F32),
            pltpu.VMEM((branches, *vec), F32),
            pltpu.VMEM((tops, *vec), F32),
            pltpu.VMEM((cut, *vec), F32),
            pltpu.VMEM((cut, *vec), F32),
            pltpu.VMEM((cut, ROWS, LANES), F32),
            pltpu.VMEM((LANES, LANES), F32),
            pltpu.VMEM((LANES, LANES), F32),
        ],
        compiler_params=pltpu.CompilerParams(vmem_limit_bytes=32 * 1024 * 1024),
        name="prune",
    )(
        leaf_order,
        me.reshape(1),
        site_weights.reshape(1, -1),
        branch_length.reshape(1, -1),
        direction.reshape(1, -1),
        *pieces,
    )


def unpack_plain(piece_refs, wide_ref, me, rows):
    (pieces,) = piece_refs
    for number in range(pieces.shape[0]):
        wide_ref[number * rows : (number + 1) * rows, :] = pieces[number].astype(F32)


def unpack_pairs(piece_refs, wide_ref, me, rows, order):
    own, *got, take = piece_refs
    deep = own.shape[1]
    here = pl.ds(pl.multiple_of(lax.rem(me, 2) * deep, deep), deep)

    def put(number, block):
        wide_ref[number * rows : (number + 1) * rows, :] = block.astype(F32).reshape(rows, LANES)

    put(0, own[...])
    put(1, take[0])
    for number, (apart, block) in enumerate(zip(order, got), 1):
        put(2 * apart, block[:, here, :])
        put(2 * apart + 1, take[number])


def by_tile(tip_probs):
    tips, states, sites = tip_probs.shape
    tiles = sites // LANES
    shaped = tip_probs.transpose(1, 0, 2).reshape(states, tips, tiles, LANES)
    return shaped.transpose(0, 2, 1, 3).reshape(states, tiles * tips, LANES)


def exchange_plain(probs):
    peers = lax.axis_size("sites")
    states, rows, _ = probs.shape
    blocks = probs.reshape(states, peers, rows // peers, LANES).transpose(1, 0, 2, 3)
    arrived = lax.all_to_all(blocks, "sites", 0, 0, tiled=True)
    return [arrived.reshape(peers, -1, LANES)], unpack_plain


def exchange_pairs(probs):
    peers = lax.axis_size("sites")
    chips, me = peers // 2, lax.axis_index("sites")
    chip, core = me // 2, me % 2
    states, rows, _ = probs.shape
    deep = rows // peers

    def cut(block, first, count):
        return lax.dynamic_slice(block, (0, first, 0), (states, count, LANES))

    far, near = range(chips // 2, chips), [*range(2, chips // 2), 1]
    order = [far[0], *(apart for pair in zip(near, far[1:]) for apart in pair)]
    got = []
    for apart in order:
        swap = [(i, i ^ (2 * apart)) for i in range(peers)]
        got.append(lax.ppermute(cut(probs, 2 * deep * (chip ^ apart), 2 * deep), "sites", swap))
    give = [cut(probs, deep * (me ^ 1), deep)] + [cut(block, deep * (1 - core), deep) for block in got]
    take = lax.ppermute(jnp.stack(give), "sites", [(i, i ^ 1) for i in range(peers)])
    return [cut(probs, deep * me, deep), *got, take], functools.partial(unpack_pairs, order=order)


def total_over_sites(part):
    peers = lax.axis_size("sites")
    rounds, bit = [[1], [3]], 4
    while bit < peers:
        if 2 * bit < peers:
            rounds.append([bit + 1, 2 * bit + 1, 3 * bit + 1])
        else:
            rounds.append([bit + 1])
        bit *= 4
    for apart in rounds:
        got = [lax.ppermute(part, "sites", [(i, i ^ step) for i in range(peers)]) for step in apart]
        part = part + got[0]
        if len(got) > 1:
            part = part + (got[1] + got[2])
    return part


def local(tip_probs, leaf_order, site_weights, branch_length, direction):
    branches = branch_length.shape[0]
    each, states, _ = tip_probs.shape
    probs = by_tile(tip_probs)
    if 4 * each % 16 == 0:
        me = lax.axis_index("sites").astype(jnp.int32)
        pieces, unpack = exchange_pairs(probs)
    else:
        me = jnp.zeros((), jnp.int32)
        pieces, unpack = exchange_plain(probs)
    part = prune(pieces, me, unpack, leaf_order, site_weights, branch_length, direction, states, each)
    sums = total_over_sites(part)[:, :branches]
    return sums[0] / sums[2] - states / (states - 1.0), sums[1] / sums[2]


def solution(mesh):
    return jax.shard_map(
        local,
        mesh=mesh,
        in_specs=(
            P(("groups", "sites"), None, None),
            P("groups"),
            P(("groups", "sites")),
            P("groups"),
            P("groups"),
        ),
        out_specs=(P("groups"), P("groups")),
        check_vma=False,
    )
```

```python
import functools
import jax
import jax.numpy as jnp
from jax import lax
from jax.experimental import pallas as pl
from jax.experimental.pallas import tpu as pltpu
from jax.sharding import PartitionSpec as P

F32 = jnp.float32
LANES = 128
ROWS = 8


def part_sum(x):
    parts = [x[i] for i in range(len(x))]
    while len(parts) > 1:
        parts = [sum(parts[i + 1 : i + 2], parts[i]) for i in range(0, len(parts), 2)]
    return parts[0]


def both(half):
    return half + pltpu.roll(half, half.shape[0] // 2, 0)


def prune_kernel(
    order_ref, me_ref, *refs, unpack, held, tips, states, each
):
    (weight_ref, length_ref, toward_ref), piece_refs = refs[:3], refs[3 : 3 + held]
    out_ref, wide_ref, *refs = refs[3 + held :]
    (
        rate_ref, slope_ref, sums_ref, dsums_ref, y_ref, dy_ref, adj_ref, dadj_ref, norm_ref, grad_ref, curve_ref,
    ) = refs
    rows = states * 4
    me = me_ref[0]
    unpack(piece_refs, wide_ref, me, each * rows)
    blocks = states * 4 // ROWS
    decay = states / (states - 1.0)
    branches = length_ref.shape[1]
    length = length_ref[...]
    toward = toward_ref[...]
    grow = jnp.exp(decay * length)
    pad = LANES - branches

    def column(row):
        wide = jnp.concatenate([row, jnp.zeros((1, pad), F32)], axis=1)
        return jnp.transpose(jnp.broadcast_to(wide, (LANES, LANES)))

    rate_ref[...] = column((grow - 1.0) / states)
    slope_ref[...] = column(decay * toward * grow / states)
    unused = jnp.zeros((grad_ref.shape[0] - branches * ROWS, LANES), F32)
    grad_ref[branches * ROWS :, :] = unused
    curve_ref[branches * ROWS :, :] = unused
    raw = weight_ref[...].astype(F32)
    quarter = [raw[:, part * LANES : (part + 1) * LANES] for part in range(4)]
    weight = jnp.concatenate(quarter + quarter, axis=0)

    offsets = [0]
    size = tips
    while size > 1:
        offsets.append(offsets[-1] + size)
        size //= 2

    def row(ref, at):
        return jnp.broadcast_to(ref[pl.ds(at, 1), :], (ROWS, LANES))

    def leaf(slot):
        tip = order_ref[slot]
        first = ((tip // each) ^ me) * (each * rows) + tip % each
        x = wide_ref[pl.ds(first, rows, each), :].reshape(blocks, ROWS, LANES)
        total = both(part_sum(x))
        lift = row(rate_ref, tip) * total
        y = x + lift[None]
        y_ref[slot] = y
        sums_ref[slot] = total
        return y, row(slope_ref, tip) * total, total + states * lift

    def cherry(k):
        ya, qa, ta = leaf(2 * k)
        yb, qb, tb = leaf(2 * k + 1)
        z = ya * yb
        dz = qa[None] * yb + qb[None] * ya
        return z, dz, both(part_sum(z)), qa * tb + qb * ta

    def inner(at, z, dz, total, dtotal):
        rate, slope = row(rate_ref, at), row(slope_ref, at)
        y = z + (rate * total)[None]
        dy = dz + (rate * dtotal + slope * total)[None]
        y_ref[at] = y
        dy_ref[at - tips] = dy
        sums_ref[at] = total
        dsums_ref[at - tips] = dtotal
        return y, dy

    def join(left, right):
        (ya, dya), (yb, dyb) = left, right
        z = ya * yb
        dz = dya * yb + ya * dyb
        return z, dz, both(part_sum(z)), both(part_sum(dz))

    def climb(level, k, low):
        if level == 1:
            return cherry(k)
        kids = []
        for child in (2 * k, 2 * k + 1):
            kids.append(inner(offsets[level - 1] + child, *climb(level - 1, child, low)))
        return join(*kids)

    levels = len(offsets) - 1
    cut = 3

    def up(k, carry):
        z, dz, total, dtotal = climb(cut, k, 0)
        scale = states / total
        norm_ref[k] = scale
        inner(offsets[cut] + k, z * scale[None], dz * scale[None], jnp.full_like(total, states), dtotal * scale)
        return carry

    lax.fori_loop(0, tips >> cut, up, 0)

    def fetch(at):
        return y_ref[at], dy_ref[at - tips]

    def climb_top(level, k):
        if level == cut:
            return fetch(offsets[cut] + k)
        kids = [climb_top(level - 1, 2 * k), climb_top(level - 1, 2 * k + 1)]
        raw_values = join(*kids)
        if level == levels:
            return raw_values
        return inner(offsets[level] + k, *raw_values)

    _, _, total, dtotal = climb_top(levels, 0)
    seed = 1.0 / total
    dseed = -(dtotal * seed) * seed

    def record(at, grad, curve):
        here = pl.ds(pl.multiple_of(at * ROWS, ROWS), ROWS)
        grad_ref[here, :] = weight * grad
        curve_ref[here, :] = weight * curve

    def down(at, ybar, dybar):
        half, dhalf = part_sum(ybar), part_sum(dybar)
        total, dtotal = sums_ref[at], dsums_ref[at - tips]
        record(at, total * half, dtotal * half + total * dhalf)
        full, dfull = both(half), both(dhalf)
        rate, slope = row(rate_ref, at), row(slope_ref, at)
        xbar = ybar + (rate * full)[None]
        dxbar = dybar + (rate * dfull + slope * full)[None]
        return xbar, dxbar, full * (1.0 + states * rate)

    def split(level, k, zbar, dzbar, zsum, low, emit):
        first, second = 2 * k, 2 * k + 1
        for child, other in ((first, second), (second, first)):
            if level == 1:
                yb = y_ref[other]
                half, dhalf = part_sum(zbar * yb), part_sum(dzbar * yb)
                tip, mate = order_ref[child], order_ref[other]
                total = sums_ref[child]
                push = row(slope_ref, mate) * sums_ref[other]
                record(tip, total * half, total * (dhalf + 0.5 * (push * zsum)))
                continue
            at, mate = offsets[level - 1] + child, offsets[level - 1] + other
            yb, dyb = fetch(mate)
            xbar, dxbar, xsum = down(at, zbar * yb, dzbar * yb + zbar * dyb)
            if level - 1 == low:
                emit(child, xbar, dxbar)
            else:
                split(level - 1, child, xbar, dxbar, xsum, low, emit)

    def keep(k, xbar, dxbar):
        scale = norm_ref[k][None]
        adj_ref[k] = xbar * scale
        dadj_ref[k] = dxbar * scale

    wide = (blocks, ROWS, LANES)
    split(levels, 0, jnp.broadcast_to(seed[None], wide), jnp.broadcast_to(dseed[None], wide), None, cut, keep)

    def descend(k, carry):
        split(cut, k, adj_ref[k], dadj_ref[k], None, 0, None)
        return carry

    lax.fori_loop(0, tips >> cut, descend, 0)

    scale = decay * grow / states

    def over_sites(ref):
        rows = part_sum([ref[pl.ds(part, LANES, ROWS), :] for part in range(ROWS)])
        return jnp.sum(jnp.transpose(rows), axis=0, keepdims=True)[:, :branches] * scale

    grad, curve = over_sites(grad_ref), over_sites(curve_ref)
    curve = curve + decay * toward * grad
    out_ref[...] = jnp.zeros_like(out_ref)
    out_ref[0:1, :branches] = grad
    out_ref[1:2, :branches] = curve
    out_ref[2:3, :] = jnp.broadcast_to(jnp.sum(0.5 * weight), (1, LANES))


def prune(pieces, me, unpack, leaf_order, site_weights, branch_length, direction, states, each):
    tips = leaf_order.shape[0]
    blocks = states * 4 // ROWS
    branches = branch_length.shape[0]
    tops = branches - tips
    cut = tips >> 3
    vm = pl.BlockSpec(memory_space=pltpu.VMEM)
    sm = pl.BlockSpec(memory_space=pltpu.SMEM)
    vec = (blocks, ROWS, LANES)
    return pl.pallas_call(
        functools.partial(
            prune_kernel, unpack=unpack, held=len(pieces), tips=tips, states=states, each=each
        ),
        in_specs=[sm, sm] + [vm] * (3 + len(pieces)),
        out_specs=vm,
        out_shape=jax.ShapeDtypeStruct((ROWS, LANES), F32),
        scratch_shapes=[
            pltpu.VMEM((tips * states * 4, LANES), F32),
            pltpu.VMEM((LANES, LANES), F32),
            pltpu.VMEM((LANES, LANES), F32),
            pltpu.VMEM((branches, ROWS, LANES), F32),
            pltpu.VMEM((tops, ROWS, LANES), F32),
            pltpu.VMEM((branches, *vec), F32),
            pltpu.VMEM((tops, *vec), F32),
            pltpu.VMEM((cut, *vec), F32),
            pltpu.VMEM((cut, *vec), F32),
            pltpu.VMEM((cut, ROWS, LANES), F32),
            pltpu.VMEM((LANES * ROWS, LANES), F32),
            pltpu.VMEM((LANES * ROWS, LANES), F32),
        ],
        compiler_params=pltpu.CompilerParams(vmem_limit_bytes=32 * 1024 * 1024),
        name="prune",
    )(
        leaf_order,
        me.reshape(1),
        site_weights.reshape(1, -1),
        branch_length.reshape(1, -1),
        direction.reshape(1, -1),
        *pieces,
    )


def unpack_plain(piece_refs, wide_ref, me, rows):
    (pieces,) = piece_refs
    for number in range(pieces.shape[0]):
        wide_ref[number * rows : (number + 1) * rows, :] = pieces[number].astype(F32)


def unpack_pairs(piece_refs, wide_ref, me, rows, order):
    own, *got, take = piece_refs
    deep = own.shape[1]
    here = pl.ds(pl.multiple_of(lax.rem(me, 2) * deep, deep), deep)

    def put(number, block):
        wide_ref[number * rows : (number + 1) * rows, :] = block.astype(F32).reshape(rows, LANES)

    put(0, own[...])
    put(1, take[0])
    for number, (apart, block) in enumerate(zip(order, got), 1):
        put(2 * apart, block[:, here, :])
        put(2 * apart + 1, take[number])


def by_tile(tip_probs):
    tips, states, sites = tip_probs.shape
    tiles = sites // LANES
    shaped = tip_probs.transpose(1, 0, 2).reshape(states, tips, tiles, LANES)
    return shaped.transpose(0, 2, 1, 3).reshape(states, tiles * tips, LANES)


def exchange_plain(probs):
    peers = lax.axis_size("sites")
    states, rows, _ = probs.shape
    blocks = probs.reshape(states, peers, rows // peers, LANES).transpose(1, 0, 2, 3)
    arrived = lax.all_to_all(blocks, "sites", 0, 0, tiled=True)
    return [arrived.reshape(peers, -1, LANES)], unpack_plain


def exchange_pairs(probs):
    peers = lax.axis_size("sites")
    chips, me = peers // 2, lax.axis_index("sites")
    chip, core = me // 2, me % 2
    states, rows, _ = probs.shape
    deep = rows // peers

    def cut(block, first, count):
        return lax.dynamic_slice(block, (0, first, 0), (states, count, LANES))

    far, near = range(chips // 2, chips), [*range(2, chips // 2), 1]
    order = [far[0], *(apart for pair in zip(near, far[1:]) for apart in pair)]
    got = []
    for apart in order:
        swap = [(i, i ^ (2 * apart)) for i in range(peers)]
        got.append(lax.ppermute(cut(probs, 2 * deep * (chip ^ apart), 2 * deep), "sites", swap))
    give = [cut(probs, deep * (me ^ 1), deep)] + [cut(block, deep * (1 - core), deep) for block in got]
    take = lax.ppermute(jnp.stack(give), "sites", [(i, i ^ 1) for i in range(peers)])
    return [cut(probs, deep * me, deep), *got, take], functools.partial(unpack_pairs, order=order)


def total_over_sites(part):
    peers = lax.axis_size("sites")
    steps, bit = [2, peers - 4], 4
    while bit < peers // 2:
        steps.append(bit)
        bit *= 2
    rounds = [[1]]
    for first in range(0, len(steps), 2):
        pair = steps[first : first + 2]
        rounds.append([step + 1 for step in ([*pair, pair[0] ^ pair[1]] if len(pair) > 1 else pair)])
    for apart in rounds:
        got = [lax.ppermute(part, "sites", [(i, i ^ step) for i in range(peers)]) for step in apart]
        part = part + got[0]
        if len(got) > 1:
            part = part + (got[1] + got[2])
    return part


def local(tip_probs, leaf_order, site_weights, branch_length, direction):
    branches = branch_length.shape[0]
    each, states, _ = tip_probs.shape
    probs = by_tile(tip_probs)
    if 4 * each % 16 == 0:
        me = lax.axis_index("sites").astype(jnp.int32)
        pieces, unpack = exchange_pairs(probs)
    else:
        me = jnp.zeros((), jnp.int32)
        pieces, unpack = exchange_plain(probs)
    part = prune(pieces, me, unpack, leaf_order, site_weights, branch_length, direction, states, each)
    sums = total_over_sites(part)[:, :branches]
    return sums[0] / sums[2] - states / (states - 1.0), sums[1] / sums[2]


def solution(mesh):
    return jax.shard_map(
        local,
        mesh=mesh,
        in_specs=(
            P(("groups", "sites"), None, None),
            P("groups"),
            P(("groups", "sites")),
            P("groups"),
            P("groups"),
        ),
        out_specs=(P("groups"), P("groups")),
        check_vma=False,
    )
```

```python
import functools
import jax
import jax.numpy as jnp
from jax import lax
from jax.experimental import pallas as pl
from jax.experimental.pallas import tpu as pltpu
from jax.sharding import PartitionSpec as P

F32 = jnp.float32
LANES = 128
ROWS = 8


def part_sum(x):
    parts = [x[i] for i in range(len(x))]
    while len(parts) > 1:
        parts = [sum(parts[i + 1 : i + 2], parts[i]) for i in range(0, len(parts), 2)]
    return parts[0]


def both(half):
    return half + pltpu.roll(half, half.shape[0] // 2, 0)


def prune_kernel(
    order_ref, me_ref, *refs, unpack, held, tips, states, each
):
    (weight_ref, length_ref, toward_ref), piece_refs = refs[:3], refs[3 : 3 + held]
    out_ref, wide_ref, *refs = refs[3 + held :]
    (
        rate_ref, slope_ref, sums_ref, dsums_ref, y_ref, dy_ref, adj_ref, dadj_ref, norm_ref, grad_ref, curve_ref,
    ) = refs
    rows = states * 4
    me = me_ref[0]
    unpack(piece_refs, wide_ref, me, each * rows)
    blocks = states * 4 // ROWS
    decay = states / (states - 1.0)
    branches = length_ref.shape[1]
    length = length_ref[...]
    toward = toward_ref[...]
    grow = jnp.exp(decay * length)
    pad = LANES - branches

    def column(row):
        wide = jnp.concatenate([row, jnp.zeros((1, pad), F32)], axis=1)
        return jnp.transpose(jnp.broadcast_to(wide, (LANES, LANES)))

    rate_ref[...] = column((grow - 1.0) / states)
    slope_ref[...] = column(decay * toward * grow / states)
    unused = jnp.zeros((grad_ref.shape[0] - branches * ROWS, LANES), F32)
    grad_ref[branches * ROWS :, :] = unused
    curve_ref[branches * ROWS :, :] = unused
    raw = weight_ref[...].astype(F32)
    quarter = [raw[:, part * LANES : (part + 1) * LANES] for part in range(4)]
    weight = jnp.concatenate(quarter + quarter, axis=0)

    offsets = [0]
    size = tips
    while size > 1:
        offsets.append(offsets[-1] + size)
        size //= 2

    def row(ref, at):
        return jnp.broadcast_to(ref[pl.ds(at, 1), :], (ROWS, LANES))

    def leaf(slot):
        tip = order_ref[slot]
        first = ((tip // each) ^ me) * (each * rows) + tip % each
        x = wide_ref[pl.ds(first, rows, each), :].reshape(blocks, ROWS, LANES)
        total = both(part_sum(x))
        lift = row(rate_ref, tip) * total
        y = x + lift[None]
        y_ref[slot] = y
        sums_ref[slot] = total
        return y, row(slope_ref, tip) * total, total + states * lift

    def cherry(k):
        ya, qa, ta = leaf(2 * k)
        yb, qb, tb = leaf(2 * k + 1)
        z = ya * yb
        dz = qa[None] * yb + qb[None] * ya
        return z, dz, both(part_sum(z)), qa * tb + qb * ta

    def inner(at, z, dz, total, dtotal):
        rate, slope = row(rate_ref, at), row(slope_ref, at)
        y = z + (rate * total)[None]
        dy = dz + (rate * dtotal + slope * total)[None]
        y_ref[at] = y
        dy_ref[at - tips] = dy
        sums_ref[at] = total
        dsums_ref[at - tips] = dtotal
        return y, dy

    def join(left, right):
        (ya, dya), (yb, dyb) = left, right
        z = ya * yb
        dz = dya * yb + ya * dyb
        return z, dz, both(part_sum(z)), both(part_sum(dz))

    def climb(level, k, low):
        if level == 1:
            return cherry(k)
        kids = []
        for child in (2 * k, 2 * k + 1):
            kids.append(inner(offsets[level - 1] + child, *climb(level - 1, child, low)))
        return join(*kids)

    levels = len(offsets) - 1
    cut = 3

    def up(k, carry):
        z, dz, total, dtotal = climb(cut, k, 0)
        scale = states / total
        norm_ref[k] = scale
        inner(offsets[cut] + k, z * scale[None], dz * scale[None], jnp.full_like(total, states), dtotal * scale)
        return carry

    lax.fori_loop(0, tips >> cut, up, 0)

    def fetch(at):
        return y_ref[at], dy_ref[at - tips]

    def climb_top(level, k):
        if level == cut:
            return fetch(offsets[cut] + k)
        kids = [climb_top(level - 1, 2 * k), climb_top(level - 1, 2 * k + 1)]
        raw_values = join(*kids)
        if level == levels:
            return raw_values
        return inner(offsets[level] + k, *raw_values)

    _, _, total, dtotal = climb_top(levels, 0)
    seed = 1.0 / total
    dseed = -(dtotal * seed) * seed

    def record(at, grad, curve):
        here = pl.ds(pl.multiple_of(at * ROWS, ROWS), ROWS)
        grad_ref[here, :] = weight * grad
        curve_ref[here, :] = weight * curve

    def down(at, ybar, dybar):
        half, dhalf = part_sum(ybar), part_sum(dybar)
        total, dtotal = sums_ref[at], dsums_ref[at - tips]
        record(at, total * half, dtotal * half + total * dhalf)
        full, dfull = both(half), both(dhalf)
        rate, slope = row(rate_ref, at), row(slope_ref, at)
        xbar = ybar + (rate * full)[None]
        dxbar = dybar + (rate * dfull + slope * full)[None]
        return xbar, dxbar, full * (1.0 + states * rate)

    def split(level, k, zbar, dzbar, zsum, low, emit):
        first, second = 2 * k, 2 * k + 1
        for child, other in ((first, second), (second, first)):
            if level == 1:
                yb = y_ref[other]
                half, dhalf = part_sum(zbar * yb), part_sum(dzbar * yb)
                tip, mate = order_ref[child], order_ref[other]
                total = sums_ref[child]
                push = row(slope_ref, mate) * sums_ref[other]
                record(tip, total * half, total * (dhalf + 0.5 * (push * zsum)))
                continue
            at, mate = offsets[level - 1] + child, offsets[level - 1] + other
            yb, dyb = fetch(mate)
            xbar, dxbar, xsum = down(at, zbar * yb, dzbar * yb + zbar * dyb)
            if level - 1 == low:
                emit(child, xbar, dxbar)
            else:
                split(level - 1, child, xbar, dxbar, xsum, low, emit)

    def keep(k, xbar, dxbar):
        scale = norm_ref[k][None]
        adj_ref[k] = xbar * scale
        dadj_ref[k] = dxbar * scale

    wide = (blocks, ROWS, LANES)
    split(levels, 0, jnp.broadcast_to(seed[None], wide), jnp.broadcast_to(dseed[None], wide), None, cut, keep)

    def descend(k, carry):
        split(cut, k, adj_ref[k], dadj_ref[k], None, 0, None)
        return carry

    lax.fori_loop(0, tips >> cut, descend, 0)

    scale = decay * grow / states

    def over_sites(ref):
        rows = part_sum([ref[pl.ds(part, LANES, ROWS), :] for part in range(ROWS)])
        return jnp.sum(jnp.transpose(rows), axis=0, keepdims=True)[:, :branches] * scale

    grad, curve = over_sites(grad_ref), over_sites(curve_ref)
    curve = curve + decay * toward * grad
    out_ref[...] = jnp.zeros_like(out_ref)
    out_ref[0:1, :branches] = grad
    out_ref[1:2, :branches] = curve
    out_ref[2:3, :] = jnp.broadcast_to(jnp.sum(0.5 * weight), (1, LANES))


def prune(pieces, me, unpack, leaf_order, site_weights, branch_length, direction, states, each):
    tips = leaf_order.shape[0]
    blocks = states * 4 // ROWS
    branches = branch_length.shape[0]
    tops = branches - tips
    cut = tips >> 3
    vm = pl.BlockSpec(memory_space=pltpu.VMEM)
    sm = pl.BlockSpec(memory_space=pltpu.SMEM)
    vec = (blocks, ROWS, LANES)
    return pl.pallas_call(
        functools.partial(
            prune_kernel, unpack=unpack, held=len(pieces), tips=tips, states=states, each=each
        ),
        in_specs=[sm, sm] + [vm] * (3 + len(pieces)),
        out_specs=vm,
        out_shape=jax.ShapeDtypeStruct((ROWS, LANES), F32),
        scratch_shapes=[
            pltpu.VMEM((tips * states * 4, LANES), F32),
            pltpu.VMEM((LANES, LANES), F32),
            pltpu.VMEM((LANES, LANES), F32),
            pltpu.VMEM((branches, ROWS, LANES), F32),
            pltpu.VMEM((tops, ROWS, LANES), F32),
            pltpu.VMEM((branches, *vec), F32),
            pltpu.VMEM((tops, *vec), F32),
            pltpu.VMEM((cut, *vec), F32),
            pltpu.VMEM((cut, *vec), F32),
            pltpu.VMEM((cut, ROWS, LANES), F32),
            pltpu.VMEM((LANES * ROWS, LANES), F32),
            pltpu.VMEM((LANES * ROWS, LANES), F32),
        ],
        compiler_params=pltpu.CompilerParams(vmem_limit_bytes=32 * 1024 * 1024),
        name="prune",
    )(
        leaf_order,
        me.reshape(1),
        site_weights.reshape(1, -1),
        branch_length.reshape(1, -1),
        direction.reshape(1, -1),
        *pieces,
    )


def unpack_plain(piece_refs, wide_ref, me, rows):
    (pieces,) = piece_refs
    for number in range(pieces.shape[0]):
        wide_ref[number * rows : (number + 1) * rows, :] = pieces[number].astype(F32)


def unpack_pairs(piece_refs, wide_ref, me, rows, order):
    own, *got, take = piece_refs
    deep = own.shape[1]
    here = pl.ds(pl.multiple_of(lax.rem(me, 2) * deep, deep), deep)

    def put(number, block):
        wide_ref[number * rows : (number + 1) * rows, :] = block.astype(F32).reshape(rows, LANES)

    put(0, own[...])
    put(1, take[0])
    for number, (apart, block) in enumerate(zip(order, got), 1):
        put(2 * apart, block[:, here, :])
        put(2 * apart + 1, take[number])


def by_tile(tip_probs):
    tips, states, sites = tip_probs.shape
    tiles = sites // LANES
    shaped = tip_probs.transpose(1, 0, 2).reshape(states, tips, tiles, LANES)
    return shaped.transpose(0, 2, 1, 3).reshape(states, tiles * tips, LANES)


def exchange_plain(probs):
    peers = lax.axis_size("sites")
    states, rows, _ = probs.shape
    blocks = probs.reshape(states, peers, rows // peers, LANES).transpose(1, 0, 2, 3)
    arrived = lax.all_to_all(blocks, "sites", 0, 0, tiled=True)
    return [arrived.reshape(peers, -1, LANES)], unpack_plain


def cut_kernel(me_ref, probs_ref, after_ref, *refs, firsts):
    out_refs, sems = refs[:-1], refs[-1]
    me = me_ref[0]
    copies = []
    for number, (out_ref, first) in enumerate(zip(out_refs, firsts)):
        count = out_ref.shape[1]
        start = pl.multiple_of(first(me), count)
        copies.append(pltpu.make_async_copy(probs_ref.at[:, pl.ds(start, count), :], out_ref, sems.at[number]))
    for copy in copies:
        copy.start()
    for copy in copies:
        copy.wait()


def cut(probs, me, firsts, counts, after):
    vm = pl.BlockSpec(memory_space=pltpu.VMEM)
    return pl.pallas_call(
        functools.partial(cut_kernel, firsts=firsts),
        in_specs=[pl.BlockSpec(memory_space=pltpu.SMEM), pl.BlockSpec(memory_space=pltpu.HBM), pl.BlockSpec(memory_space=pl.ANY)],
        out_specs=[vm] * len(counts),
        out_shape=[jax.ShapeDtypeStruct((probs.shape[0], count, LANES), probs.dtype) for count in counts],
        scratch_shapes=[pltpu.SemaphoreType.DMA((len(counts),))],
        compiler_params=pltpu.CompilerParams(vmem_limit_bytes=16 * 1024 * 1024),
        name="cut",
    )(me.reshape(1), pltpu.with_memory_space_constraint(probs, pltpu.HBM), after)


def exchange_pairs(probs, me):
    peers = lax.axis_size("sites")
    chips = peers // 2
    core = me % 2
    states, rows, _ = probs.shape
    deep = rows // peers
    far, near = range(chips // 2, chips), [*range(2, chips // 2), 1]
    order = [far[0], *(apart for pair in zip(near, far[1:]) for apart in pair)]
    firsts = [lambda me, apart=apart: (((me // 2) ^ apart) * (2 * deep)) for apart in order]
    firsts += [lambda me: me * deep, lambda me: (me ^ 1) * deep]
    counts = [2 * deep] * len(order) + [deep] * 2
    head = cut(probs, me, firsts[:1], counts[:1], me.reshape(1))
    *tail, own, spare = cut(probs, me, firsts[1:], counts[1:], head[0])
    sent = [*head, *tail]
    got = []
    for apart, block in zip(order, sent):
        got.append(lax.ppermute(block, "sites", [(i, i ^ (2 * apart)) for i in range(peers)]))
    other = deep * (1 - core)
    give = [spare] + [lax.dynamic_slice(block, (0, other, 0), (states, deep, LANES)) for block in got]
    take = lax.ppermute(jnp.stack(give), "sites", [(i, i ^ 1) for i in range(peers)])
    return [own, *got, take], functools.partial(unpack_pairs, order=order)


def total_over_sites(part):
    peers = lax.axis_size("sites")
    steps, bit = [2, peers - 4], 4
    while bit < peers // 2:
        steps.append(bit)
        bit *= 2
    rounds = [[1]]
    for first in range(0, len(steps), 2):
        pair = steps[first : first + 2]
        rounds.append([step + 1 for step in ([*pair, pair[0] ^ pair[1]] if len(pair) > 1 else pair)])
    for apart in rounds:
        got = [lax.ppermute(part, "sites", [(i, i ^ step) for i in range(peers)]) for step in apart]
        part = part + got[0]
        if len(got) > 1:
            part = part + (got[1] + got[2])
    return part


def local(tip_probs, leaf_order, site_weights, branch_length, direction):
    branches = branch_length.shape[0]
    each, states, _ = tip_probs.shape
    probs = by_tile(tip_probs)
    if 4 * each % 16 == 0:
        me = lax.axis_index("sites").astype(jnp.int32)
        pieces, unpack = exchange_pairs(probs, me)
    else:
        me = jnp.zeros((), jnp.int32)
        pieces, unpack = exchange_plain(probs)
    part = prune(pieces, me, unpack, leaf_order, site_weights, branch_length, direction, states, each)
    sums = total_over_sites(part)[:, :branches]
    return sums[0] / sums[2] - states / (states - 1.0), sums[1] / sums[2]


def solution(mesh):
    return jax.shard_map(
        local,
        mesh=mesh,
        in_specs=(
            P(("groups", "sites"), None, None),
            P("groups"),
            P(("groups", "sites")),
            P("groups"),
            P("groups"),
        ),
        out_specs=(P("groups"), P("groups")),
        check_vma=False,
    )
```

```python
import functools
import jax
import jax.numpy as jnp
from jax import lax
from jax.experimental import pallas as pl
from jax.experimental.pallas import tpu as pltpu
from jax.sharding import PartitionSpec as P

F32 = jnp.float32
LANES = 128
ROWS = 8


def part_sum(x):
    parts = [x[i] for i in range(len(x))]
    while len(parts) > 1:
        parts = [sum(parts[i + 1 : i + 2], parts[i]) for i in range(0, len(parts), 2)]
    return parts[0]


def both(half):
    return half + pltpu.roll(half, half.shape[0] // 2, 0)


def prune_kernel(
    order_ref, me_ref, *refs, unpack, held, tips, states, each
):
    (weight_ref, length_ref, toward_ref), piece_refs = refs[:3], refs[3 : 3 + held]
    out_ref, wide_ref, *refs = refs[3 + held :]
    (
        rate_ref, slope_ref, sums_ref, dsums_ref, y_ref, dy_ref, adj_ref, dadj_ref, norm_ref, grad_ref, curve_ref,
    ) = refs
    rows = states * 4
    me = me_ref[0]
    unpack(piece_refs, wide_ref, me, each * rows)
    blocks = states * 4 // ROWS
    decay = states / (states - 1.0)
    branches = length_ref.shape[1]
    length = length_ref[...]
    toward = toward_ref[...]
    grow = jnp.exp(decay * length)
    pad = LANES - branches

    def column(row):
        wide = jnp.concatenate([row, jnp.zeros((1, pad), F32)], axis=1)
        return jnp.transpose(jnp.broadcast_to(wide, (LANES, LANES)))

    rate_ref[...] = column((grow - 1.0) / states)
    slope_ref[...] = column(decay * toward * grow / states)
    unused = jnp.zeros((grad_ref.shape[0] - branches * ROWS, LANES), F32)
    grad_ref[branches * ROWS :, :] = unused
    curve_ref[branches * ROWS :, :] = unused
    raw = weight_ref[...].astype(F32)
    quarter = [raw[:, part * LANES : (part + 1) * LANES] for part in range(4)]
    weight = jnp.concatenate(quarter + quarter, axis=0)

    offsets = [0]
    size = tips
    while size > 1:
        offsets.append(offsets[-1] + size)
        size //= 2

    def row(ref, at):
        return jnp.broadcast_to(ref[pl.ds(at, 1), :], (ROWS, LANES))

    def leaf(slot):
        tip = order_ref[slot]
        first = ((tip // each) ^ me) * (each * rows) + tip % each
        x = wide_ref[pl.ds(first, rows, each), :].reshape(blocks, ROWS, LANES)
        total = both(part_sum(x))
        lift = row(rate_ref, tip) * total
        y = x + lift[None]
        y_ref[slot] = y
        sums_ref[slot] = total
        return y, row(slope_ref, tip) * total, total + states * lift

    def cherry(k):
        ya, qa, ta = leaf(2 * k)
        yb, qb, tb = leaf(2 * k + 1)
        z = ya * yb
        dz = qa[None] * yb + qb[None] * ya
        return z, dz, both(part_sum(z)), qa * tb + qb * ta

    def inner(at, z, dz, total, dtotal):
        rate, slope = row(rate_ref, at), row(slope_ref, at)
        y = z + (rate * total)[None]
        dy = dz + (rate * dtotal + slope * total)[None]
        y_ref[at] = y
        dy_ref[at - tips] = dy
        sums_ref[at] = total
        dsums_ref[at - tips] = dtotal
        return y, dy

    def join(left, right):
        (ya, dya), (yb, dyb) = left, right
        z = ya * yb
        dz = dya * yb + ya * dyb
        return z, dz, both(part_sum(z)), both(part_sum(dz))

    def climb(level, k, low):
        if level == 1:
            return cherry(k)
        kids = []
        for child in (2 * k, 2 * k + 1):
            kids.append(inner(offsets[level - 1] + child, *climb(level - 1, child, low)))
        return join(*kids)

    levels = len(offsets) - 1
    cut = 3

    def up(k, carry):
        z, dz, total, dtotal = climb(cut, k, 0)
        scale = states / total
        norm_ref[k] = scale
        inner(offsets[cut] + k, z * scale[None], dz * scale[None], jnp.full_like(total, states), dtotal * scale)
        return carry

    lax.fori_loop(0, tips >> cut, up, 0)

    def fetch(at):
        return y_ref[at], dy_ref[at - tips]

    def climb_top(level, k):
        if level == cut:
            return fetch(offsets[cut] + k)
        kids = [climb_top(level - 1, 2 * k), climb_top(level - 1, 2 * k + 1)]
        raw_values = join(*kids)
        if level == levels:
            return raw_values
        return inner(offsets[level] + k, *raw_values)

    _, _, total, dtotal = climb_top(levels, 0)
    seed = 1.0 / total
    dseed = -(dtotal * seed) * seed

    def record(at, grad, curve):
        here = pl.ds(pl.multiple_of(at * ROWS, ROWS), ROWS)
        grad_ref[here, :] = weight * grad
        curve_ref[here, :] = weight * curve

    def down(at, ybar, dybar):
        half, dhalf = part_sum(ybar), part_sum(dybar)
        total, dtotal = sums_ref[at], dsums_ref[at - tips]
        record(at, total * half, dtotal * half + total * dhalf)
        full, dfull = both(half), both(dhalf)
        rate, slope = row(rate_ref, at), row(slope_ref, at)
        xbar = ybar + (rate * full)[None]
        dxbar = dybar + (rate * dfull + slope * full)[None]
        return xbar, dxbar, full * (1.0 + states * rate)

    def split(level, k, zbar, dzbar, zsum, low, emit):
        first, second = 2 * k, 2 * k + 1
        for child, other in ((first, second), (second, first)):
            if level == 1:
                yb = y_ref[other]
                half, dhalf = part_sum(zbar * yb), part_sum(dzbar * yb)
                tip, mate = order_ref[child], order_ref[other]
                total = sums_ref[child]
                push = row(slope_ref, mate) * sums_ref[other]
                record(tip, total * half, total * (dhalf + 0.5 * (push * zsum)))
                continue
            at, mate = offsets[level - 1] + child, offsets[level - 1] + other
            yb, dyb = fetch(mate)
            xbar, dxbar, xsum = down(at, zbar * yb, dzbar * yb + zbar * dyb)
            if level - 1 == low:
                emit(child, xbar, dxbar)
            else:
                split(level - 1, child, xbar, dxbar, xsum, low, emit)

    def keep(k, xbar, dxbar):
        scale = norm_ref[k][None]
        adj_ref[k] = xbar * scale
        dadj_ref[k] = dxbar * scale

    wide = (blocks, ROWS, LANES)
    split(levels, 0, jnp.broadcast_to(seed[None], wide), jnp.broadcast_to(dseed[None], wide), None, cut, keep)

    def descend(k, carry):
        split(cut, k, adj_ref[k], dadj_ref[k], None, 0, None)
        return carry

    lax.fori_loop(0, tips >> cut, descend, 0)

    scale = decay * grow / states

    def over_sites(ref):
        rows = part_sum([ref[pl.ds(part, LANES, ROWS), :] for part in range(ROWS)])
        return jnp.sum(jnp.transpose(rows), axis=0, keepdims=True)[:, :branches] * scale

    grad, curve = over_sites(grad_ref), over_sites(curve_ref)
    curve = curve + decay * toward * grad
    out_ref[...] = jnp.zeros_like(out_ref)
    out_ref[0:1, :branches] = grad
    out_ref[1:2, :branches] = curve
    out_ref[2:3, :] = jnp.broadcast_to(jnp.sum(0.5 * weight), (1, LANES))


def prune(pieces, me, unpack, leaf_order, site_weights, branch_length, direction, states, each):
    tips = leaf_order.shape[0]
    blocks = states * 4 // ROWS
    branches = branch_length.shape[0]
    tops = branches - tips
    cut = tips >> 3
    vm = pl.BlockSpec(memory_space=pltpu.VMEM)
    sm = pl.BlockSpec(memory_space=pltpu.SMEM)
    vec = (blocks, ROWS, LANES)
    return pl.pallas_call(
        functools.partial(
            prune_kernel, unpack=unpack, held=len(pieces), tips=tips, states=states, each=each
        ),
        in_specs=[sm, sm] + [vm] * (3 + len(pieces)),
        out_specs=vm,
        out_shape=jax.ShapeDtypeStruct((ROWS, LANES), F32),
        scratch_shapes=[
            pltpu.VMEM((tips * states * 4, LANES), F32),
            pltpu.VMEM((LANES, LANES), F32),
            pltpu.VMEM((LANES, LANES), F32),
            pltpu.VMEM((branches, ROWS, LANES), F32),
            pltpu.VMEM((tops, ROWS, LANES), F32),
            pltpu.VMEM((branches, *vec), F32),
            pltpu.VMEM((tops, *vec), F32),
            pltpu.VMEM((cut, *vec), F32),
            pltpu.VMEM((cut, *vec), F32),
            pltpu.VMEM((cut, ROWS, LANES), F32),
            pltpu.VMEM((LANES * ROWS, LANES), F32),
            pltpu.VMEM((LANES * ROWS, LANES), F32),
        ],
        compiler_params=pltpu.CompilerParams(vmem_limit_bytes=32 * 1024 * 1024),
        name="prune",
    )(
        leaf_order,
        me.reshape(1),
        site_weights.reshape(1, -1),
        branch_length.reshape(1, -1),
        direction.reshape(1, -1),
        *pieces,
    )


def unpack_plain(piece_refs, wide_ref, me, rows):
    (pieces,) = piece_refs
    for number in range(pieces.shape[0]):
        wide_ref[number * rows : (number + 1) * rows, :] = pieces[number].astype(F32)


def unpack_pairs(piece_refs, wide_ref, me, rows, order):
    own, *got, take, take_last = piece_refs
    deep = own.shape[1]
    here = pl.ds(pl.multiple_of(lax.rem(me, 2) * deep, deep), deep)

    def put(number, block):
        wide_ref[number * rows : (number + 1) * rows, :] = block.astype(F32).reshape(rows, LANES)

    put(0, own[...])
    put(1, take[0])
    for number, (apart, block) in enumerate(zip(order, got), 1):
        put(2 * apart, block[:, here, :])
        late = number - take.shape[0]
        put(2 * apart + 1, take_last[late] if late >= 0 else take[number])


def by_tile(tip_probs):
    tips, states, sites = tip_probs.shape
    tiles = sites // LANES
    shaped = tip_probs.transpose(1, 0, 2).reshape(states, tips, tiles, LANES)
    return shaped.transpose(0, 2, 1, 3).reshape(states, tiles * tips, LANES)


def exchange_plain(probs):
    peers = lax.axis_size("sites")
    states, rows, _ = probs.shape
    blocks = probs.reshape(states, peers, rows // peers, LANES).transpose(1, 0, 2, 3)
    arrived = lax.all_to_all(blocks, "sites", 0, 0, tiled=True)
    return [arrived.reshape(peers, -1, LANES)], unpack_plain


def cut_kernel(me_ref, probs_ref, after_ref, *refs, firsts):
    out_refs, sems = refs[:-1], refs[-1]
    me = me_ref[0]
    copies = []
    for number, (out_ref, first) in enumerate(zip(out_refs, firsts)):
        count = out_ref.shape[1]
        start = pl.multiple_of(first(me), count)
        copies.append(pltpu.make_async_copy(probs_ref.at[:, pl.ds(start, count), :], out_ref, sems.at[number]))
    for copy in copies:
        copy.start()
    for copy in copies:
        copy.wait()


def cut(probs, me, firsts, counts, after):
    vm = pl.BlockSpec(memory_space=pltpu.VMEM)
    return pl.pallas_call(
        functools.partial(cut_kernel, firsts=firsts),
        in_specs=[pl.BlockSpec(memory_space=pltpu.SMEM), pl.BlockSpec(memory_space=pltpu.HBM), pl.BlockSpec(memory_space=pl.ANY)],
        out_specs=[vm] * len(counts),
        out_shape=[jax.ShapeDtypeStruct((probs.shape[0], count, LANES), probs.dtype) for count in counts],
        scratch_shapes=[pltpu.SemaphoreType.DMA((len(counts),))],
        compiler_params=pltpu.CompilerParams(vmem_limit_bytes=16 * 1024 * 1024),
        name="cut",
    )(me.reshape(1), pltpu.with_memory_space_constraint(probs, pltpu.HBM), after)


def exchange_pairs(probs, me):
    peers = lax.axis_size("sites")
    chips = peers // 2
    core = me % 2
    states, rows, _ = probs.shape
    deep = rows // peers
    far, near = range(chips // 2, chips), [*range(2, chips // 2), 1]
    order = [far[0], *(apart for pair in zip(near, far[1:]) for apart in pair)]
    firsts = [lambda me, apart=apart: (((me // 2) ^ apart) * (2 * deep)) for apart in order]
    firsts += [lambda me: me * deep, lambda me: (me ^ 1) * deep]
    counts = [2 * deep] * len(order) + [deep] * 2
    head = cut(probs, me, firsts[:1], counts[:1], me.reshape(1))
    *tail, own, spare = cut(probs, me, firsts[1:], counts[1:], head[0])
    sent = [*head, *tail]
    got = []
    for apart, block in zip(order, sent):
        got.append(lax.ppermute(block, "sites", [(i, i ^ (2 * apart)) for i in range(peers)]))
    other = deep * (1 - core)
    give = [spare] + [lax.dynamic_slice(block, (0, other, 0), (states, deep, LANES)) for block in got]
    cores = [(i, i ^ 1) for i in range(peers)]
    take = lax.ppermute(jnp.stack(give[:-2]), "sites", cores)
    take_last = lax.ppermute(jnp.stack(give[-2:]), "sites", cores)
    return [own, *got, take, take_last], functools.partial(unpack_pairs, order=order)


def total_over_sites(part):
    peers = lax.axis_size("sites")
    steps, bit = [2, peers - 4], 4
    while bit < peers // 2:
        steps.append(bit)
        bit *= 2
    rounds = [[1]]
    for first in range(0, len(steps), 2):
        pair = steps[first : first + 2]
        rounds.append([step + 1 for step in ([pair[0], pair[0] ^ pair[1], pair[1]] if len(pair) > 1 else pair)])
    for apart in rounds:
        got = [lax.ppermute(part, "sites", [(i, i ^ step) for i in range(peers)]) for step in apart]
        part = part + got[0]
        if len(got) > 1:
            part = part + (got[1] + got[2])
    return part


def local(tip_probs, leaf_order, site_weights, branch_length, direction):
    branches = branch_length.shape[0]
    each, states, _ = tip_probs.shape
    probs = by_tile(tip_probs)
    if 4 * each % 16 == 0:
        me = lax.axis_index("sites").astype(jnp.int32)
        pieces, unpack = exchange_pairs(probs, me)
    else:
        me = jnp.zeros((), jnp.int32)
        pieces, unpack = exchange_plain(probs)
    part = prune(pieces, me, unpack, leaf_order, site_weights, branch_length, direction, states, each)
    sums = total_over_sites(part)[:, :branches]
    return sums[0] / sums[2] - states / (states - 1.0), sums[1] / sums[2]


def solution(mesh):
    return jax.shard_map(
        local,
        mesh=mesh,
        in_specs=(
            P(("groups", "sites"), None, None),
            P("groups"),
            P(("groups", "sites")),
            P("groups"),
            P("groups"),
        ),
        out_specs=(P("groups"), P("groups")),
        check_vma=False,
    )
```

```python
import functools
import jax
import jax.numpy as jnp
from jax import lax
from jax.experimental import pallas as pl
from jax.experimental.pallas import tpu as pltpu
from jax.sharding import PartitionSpec as P

F32 = jnp.float32
LANES = 128
ROWS = 8


def part_sum(x):
    parts = [x[i] for i in range(len(x))]
    while len(parts) > 1:
        parts = [sum(parts[i + 1 : i + 2], parts[i]) for i in range(0, len(parts), 2)]
    return parts[0]


def both(half):
    return half + pltpu.roll(half, half.shape[0] // 2, 0)


def prune_kernel(
    order_ref, me_ref, *refs, unpack, held, tips, states, each
):
    (weight_ref, length_ref, toward_ref), piece_refs = refs[:3], refs[3 : 3 + held]
    out_ref, wide_ref, *refs = refs[3 + held :]
    (
        rate_ref, slope_ref, sums_ref, dsums_ref, y_ref, dy_ref, adj_ref, dadj_ref, norm_ref, grad_ref, curve_ref,
    ) = refs
    rows = states * 4
    me = me_ref[0]
    unpack(piece_refs, wide_ref, me, each * rows)
    blocks = states * 4 // ROWS
    decay = states / (states - 1.0)
    branches = length_ref.shape[1]
    length = length_ref[...]
    toward = toward_ref[...]
    grow = jnp.exp(decay * length)
    pad = LANES - branches

    def column(row):
        wide = jnp.concatenate([row, jnp.zeros((1, pad), F32)], axis=1)
        return jnp.transpose(jnp.broadcast_to(wide, (LANES, LANES)))

    rate_ref[...] = column((grow - 1.0) / states)
    slope_ref[...] = column(decay * toward * grow / states)
    unused = jnp.zeros((grad_ref.shape[0] - branches * ROWS, LANES), F32)
    grad_ref[branches * ROWS :, :] = unused
    curve_ref[branches * ROWS :, :] = unused
    raw = weight_ref[...].astype(F32)
    quarter = [raw[:, part * LANES : (part + 1) * LANES] for part in range(4)]
    weight = jnp.concatenate(quarter + quarter, axis=0)

    offsets = [0]
    size = tips
    while size > 1:
        offsets.append(offsets[-1] + size)
        size //= 2

    def row(ref, at):
        return jnp.broadcast_to(ref[pl.ds(at, 1), :], (ROWS, LANES))

    def leaf(slot):
        tip = order_ref[slot]
        first = ((tip // each) ^ me) * (each * rows) + tip % each
        x = wide_ref[pl.ds(first, rows, each), :].reshape(blocks, ROWS, LANES)
        total = both(part_sum(x))
        lift = row(rate_ref, tip) * total
        y = x + lift[None]
        y_ref[slot] = y
        sums_ref[slot] = total
        return y, row(slope_ref, tip) * total, total + states * lift

    def cherry(k):
        ya, qa, ta = leaf(2 * k)
        yb, qb, tb = leaf(2 * k + 1)
        z = ya * yb
        dz = qa[None] * yb + qb[None] * ya
        return z, dz, both(part_sum(z)), qa * tb + qb * ta

    def inner(at, z, dz, total, dtotal):
        rate, slope = row(rate_ref, at), row(slope_ref, at)
        y = z + (rate * total)[None]
        dy = dz + (rate * dtotal + slope * total)[None]
        y_ref[at] = y
        dy_ref[at - tips] = dy
        sums_ref[at] = total
        dsums_ref[at - tips] = dtotal
        return y, dy

    def join(left, right):
        (ya, dya), (yb, dyb) = left, right
        z = ya * yb
        dz = dya * yb + ya * dyb
        return z, dz, both(part_sum(z)), both(part_sum(dz))

    def climb(level, k, low):
        if level == 1:
            return cherry(k)
        kids = []
        for child in (2 * k, 2 * k + 1):
            kids.append(inner(offsets[level - 1] + child, *climb(level - 1, child, low)))
        return join(*kids)

    levels = len(offsets) - 1
    cut = 3

    def up(k, carry):
        z, dz, total, dtotal = climb(cut, k, 0)
        scale = states / total
        norm_ref[k] = scale
        inner(offsets[cut] + k, z * scale[None], dz * scale[None], jnp.full_like(total, states), dtotal * scale)
        return carry

    lax.fori_loop(0, tips >> cut, up, 0)

    def fetch(at):
        return y_ref[at], dy_ref[at - tips]

    def climb_top(level, k):
        if level == cut:
            return fetch(offsets[cut] + k)
        kids = [climb_top(level - 1, 2 * k), climb_top(level - 1, 2 * k + 1)]
        raw_values = join(*kids)
        if level == levels:
            return raw_values
        return inner(offsets[level] + k, *raw_values)

    _, _, total, dtotal = climb_top(levels, 0)
    seed = 1.0 / total
    dseed = -(dtotal * seed) * seed

    def record(at, grad, curve):
        here = pl.ds(pl.multiple_of(at * ROWS, ROWS), ROWS)
        grad_ref[here, :] = weight * grad
        curve_ref[here, :] = weight * curve

    def down(at, ybar, dybar):
        half, dhalf = part_sum(ybar), part_sum(dybar)
        total, dtotal = sums_ref[at], dsums_ref[at - tips]
        record(at, total * half, dtotal * half + total * dhalf)
        full, dfull = both(half), both(dhalf)
        rate, slope = row(rate_ref, at), row(slope_ref, at)
        xbar = ybar + (rate * full)[None]
        dxbar = dybar + (rate * dfull + slope * full)[None]
        return xbar, dxbar, full * (1.0 + states * rate)

    def split(level, k, zbar, dzbar, zsum, low, emit):
        first, second = 2 * k, 2 * k + 1
        for child, other in ((first, second), (second, first)):
            if level == 1:
                yb = y_ref[other]
                half, dhalf = part_sum(zbar * yb), part_sum(dzbar * yb)
                tip, mate = order_ref[child], order_ref[other]
                total = sums_ref[child]
                push = row(slope_ref, mate) * sums_ref[other]
                record(tip, total * half, total * (dhalf + 0.5 * (push * zsum)))
                continue
            at, mate = offsets[level - 1] + child, offsets[level - 1] + other
            yb, dyb = fetch(mate)
            xbar, dxbar, xsum = down(at, zbar * yb, dzbar * yb + zbar * dyb)
            if level - 1 == low:
                emit(child, xbar, dxbar)
            else:
                split(level - 1, child, xbar, dxbar, xsum, low, emit)

    def keep(k, xbar, dxbar):
        scale = norm_ref[k][None]
        adj_ref[k] = xbar * scale
        dadj_ref[k] = dxbar * scale

    wide = (blocks, ROWS, LANES)
    split(levels, 0, jnp.broadcast_to(seed[None], wide), jnp.broadcast_to(dseed[None], wide), None, cut, keep)

    def descend(k, carry):
        split(cut, k, adj_ref[k], dadj_ref[k], None, 0, None)
        return carry

    lax.fori_loop(0, tips >> cut, descend, 0)

    scale = decay * grow / states

    def over_sites(ref):
        rows = part_sum([ref[pl.ds(part, LANES, ROWS), :] for part in range(ROWS)])
        return jnp.sum(jnp.transpose(rows), axis=0, keepdims=True)[:, :branches] * scale

    grad, curve = over_sites(grad_ref), over_sites(curve_ref)
    curve = curve + decay * toward * grad
    out_ref[...] = jnp.zeros_like(out_ref)
    out_ref[0:1, :branches] = grad
    out_ref[1:2, :branches] = curve
    out_ref[2:3, :] = jnp.broadcast_to(jnp.sum(0.5 * weight), (1, LANES))


def prune(pieces, me, unpack, leaf_order, site_weights, branch_length, direction, states, each):
    tips = leaf_order.shape[0]
    blocks = states * 4 // ROWS
    branches = branch_length.shape[0]
    tops = branches - tips
    cut = tips >> 3
    vm = pl.BlockSpec(memory_space=pltpu.VMEM)
    sm = pl.BlockSpec(memory_space=pltpu.SMEM)
    vec = (blocks, ROWS, LANES)
    return pl.pallas_call(
        functools.partial(
            prune_kernel, unpack=unpack, held=len(pieces), tips=tips, states=states, each=each
        ),
        in_specs=[sm, sm] + [vm] * (3 + len(pieces)),
        out_specs=vm,
        out_shape=jax.ShapeDtypeStruct((ROWS, LANES), F32),
        scratch_shapes=[
            pltpu.VMEM((tips * states * 4, LANES), F32),
            pltpu.VMEM((LANES, LANES), F32),
            pltpu.VMEM((LANES, LANES), F32),
            pltpu.VMEM((branches, ROWS, LANES), F32),
            pltpu.VMEM((tops, ROWS, LANES), F32),
            pltpu.VMEM((branches, *vec), F32),
            pltpu.VMEM((tops, *vec), F32),
            pltpu.VMEM((cut, *vec), F32),
            pltpu.VMEM((cut, *vec), F32),
            pltpu.VMEM((cut, ROWS, LANES), F32),
            pltpu.VMEM((LANES * ROWS, LANES), F32),
            pltpu.VMEM((LANES * ROWS, LANES), F32),
        ],
        compiler_params=pltpu.CompilerParams(vmem_limit_bytes=32 * 1024 * 1024),
        name="prune",
    )(
        leaf_order,
        me.reshape(1),
        site_weights.reshape(1, -1),
        branch_length.reshape(1, -1),
        direction.reshape(1, -1),
        *pieces,
    )


def unpack_plain(piece_refs, wide_ref, me, rows):
    (pieces,) = piece_refs
    for number in range(pieces.shape[0]):
        wide_ref[number * rows : (number + 1) * rows, :] = pieces[number].astype(F32)


def unpack_pairs(piece_refs, wide_ref, me, rows, early, late):
    own, first, *refs = piece_refs
    deep = own.shape[1]
    here = pl.ds(pl.multiple_of(lax.rem(me, 2) * deep, deep), deep)

    def put(number, block):
        wide_ref[number * rows : (number + 1) * rows, :] = block.astype(F32).reshape(rows, LANES)

    put(0, own[...])
    put(1, first[0])
    both_refs, late_refs, swapped_refs = refs[: len(early)], refs[len(early) :][: len(late)], refs[len(early) + len(late) :]
    for apart, block in zip(early, both_refs):
        put(2 * apart, block[:, here, :])
    for apart, block in zip(late, late_refs):
        put(2 * apart, block[0])
        put(2 * apart + 1, block[1])
    for number, apart in enumerate(early):
        block = swapped_refs[number // 2]
        put(2 * apart + 1, block[number % 2])


def by_tile(tip_probs):
    tips, states, sites = tip_probs.shape
    tiles = sites // LANES
    shaped = tip_probs.transpose(1, 0, 2).reshape(states, tips, tiles, LANES)
    return shaped.transpose(0, 2, 1, 3).reshape(states, tiles * tips, LANES)


def exchange_plain(probs):
    peers = lax.axis_size("sites")
    states, rows, _ = probs.shape
    blocks = probs.reshape(states, peers, rows // peers, LANES).transpose(1, 0, 2, 3)
    arrived = lax.all_to_all(blocks, "sites", 0, 0, tiled=True)
    return [arrived.reshape(peers, -1, LANES)], unpack_plain


def cut_kernel(me_ref, probs_ref, after_ref, *refs, firsts):
    out_refs, sems = refs[:-1], refs[-1]
    me = me_ref[0]
    copies = []
    for out_ref, places in zip(out_refs, firsts):
        for slot, first in enumerate(places):
            count = out_ref.shape[2]
            start = pl.multiple_of(first(me), count)
            source = probs_ref.at[:, pl.ds(start, count), :]
            copies.append(pltpu.make_async_copy(source, out_ref.at[slot], sems.at[len(copies)]))
    for copy in copies:
        copy.start()
    for copy in copies:
        copy.wait()


def cut(probs, me, firsts, counts, after):
    vm = pl.BlockSpec(memory_space=pltpu.VMEM)
    states = probs.shape[0]
    return pl.pallas_call(
        functools.partial(cut_kernel, firsts=firsts),
        in_specs=[
            pl.BlockSpec(memory_space=pltpu.SMEM),
            pl.BlockSpec(memory_space=pltpu.HBM),
            pl.BlockSpec(memory_space=pl.ANY),
        ],
        out_specs=[vm] * len(counts),
        out_shape=[
            jax.ShapeDtypeStruct((len(places), states, count, LANES), probs.dtype)
            for places, count in zip(firsts, counts)
        ],
        scratch_shapes=[pltpu.SemaphoreType.DMA((sum(len(places) for places in firsts),))],
        compiler_params=pltpu.CompilerParams(vmem_limit_bytes=16 * 1024 * 1024),
        name="cut",
    )(me.reshape(1), pltpu.with_memory_space_constraint(probs, pltpu.HBM), after)


def exchange_pairs(probs, me):
    peers = lax.axis_size("sites")
    chips = peers // 2
    core = me % 2
    states, rows, _ = probs.shape
    deep = rows // peers
    far, near = range(chips // 2, chips), [*range(2, chips // 2), 1]
    order = [far[0], *(apart for pair in zip(near, far[1:]) for apart in pair)]
    early, late = order[:-1], order[-1:]

    def chip_first(apart):
        return lambda me: ((me // 2) ^ apart) * (2 * deep)

    def core_first(step):
        return lambda me: (me ^ step) * deep

    firsts = [[chip_first(apart)] for apart in early]
    counts = [2 * deep] * len(early)
    head = cut(probs, me, firsts[:1], counts[:1], me.reshape(1))
    firsts += [[core_first(1), *(core_first(2 * apart + 1) for apart in late)]]
    firsts += [[core_first(2 * apart)] for apart in late]
    firsts += [[core_first(0)]]
    counts += [deep] * (len(late) + 2)
    tail = cut(probs, me, firsts[1:], counts[1:], head[0])
    sent = [*head, *tail[: len(early) - 1]]
    give, *mine, own = tail[len(early) - 1 :]

    def swap(block, step):
        return lax.ppermute(block, "sites", [(i, i ^ step) for i in range(peers)])

    first = swap(give, 1)
    got = [swap(block[0], 2 * apart) for apart, block in zip(early, sent)]
    for number, apart in enumerate(late):
        got.append(swap(jnp.concatenate([mine[number], first[number + 1 : number + 2]], axis=0), 2 * apart))
    other = deep * (1 - core)
    give = [lax.dynamic_slice(block, (0, other, 0), (states, deep, LANES)) for block in got[: len(early)]]
    swapped = [swap(jnp.stack(give[at : at + 2]), 1) for at in range(0, len(give), 2)]
    return [own[0], first, *got, *swapped], functools.partial(unpack_pairs, early=early, late=late)


def total_over_sites(part):
    peers = lax.axis_size("sites")
    steps, bit = [2, peers - 4], 4
    while bit < peers // 2:
        steps.append(bit)
        bit *= 2
    rounds = [[1]]
    for first in range(0, len(steps), 2):
        pair = steps[first : first + 2]
        rounds.append([step + 1 for step in ([*pair, pair[0] ^ pair[1]] if len(pair) > 1 else pair)])
    for apart in rounds:
        got = [lax.ppermute(part, "sites", [(i, i ^ step) for i in range(peers)]) for step in apart]
        part = part + got[0]
        if len(got) > 1:
            part = part + (got[1] + got[2])
    return part


def local(tip_probs, leaf_order, site_weights, branch_length, direction):
    branches = branch_length.shape[0]
    each, states, _ = tip_probs.shape
    probs = by_tile(tip_probs)
    if 4 * each % 16 == 0:
        me = lax.axis_index("sites").astype(jnp.int32)
        pieces, unpack = exchange_pairs(probs, me)
    else:
        me = jnp.zeros((), jnp.int32)
        pieces, unpack = exchange_plain(probs)
    part = prune(pieces, me, unpack, leaf_order, site_weights, branch_length, direction, states, each)
    sums = total_over_sites(part)[:, :branches]
    return sums[0] / sums[2] - states / (states - 1.0), sums[1] / sums[2]


def solution(mesh):
    return jax.shard_map(
        local,
        mesh=mesh,
        in_specs=(
            P(("groups", "sites"), None, None),
            P("groups"),
            P(("groups", "sites")),
            P("groups"),
            P("groups"),
        ),
        out_specs=(P("groups"), P("groups")),
        check_vma=False,
    )
```

```python
import functools
import jax
import jax.numpy as jnp
from jax import lax
from jax.experimental import pallas as pl
from jax.experimental.pallas import tpu as pltpu
from jax.sharding import PartitionSpec as P

F32 = jnp.float32
LANES = 128
ROWS = 8


def part_sum(x):
    parts = [x[i] for i in range(len(x))]
    while len(parts) > 1:
        parts = [sum(parts[i + 1 : i + 2], parts[i]) for i in range(0, len(parts), 2)]
    return parts[0]


def both(half):
    return half + pltpu.roll(half, half.shape[0] // 2, 0)


def prune_kernel(
    order_ref, me_ref, *refs, unpack, held, tips, states, each
):
    (weight_ref, length_ref, toward_ref), piece_refs = refs[:3], refs[3 : 3 + held]
    out_ref, wide_ref, *refs = refs[3 + held :]
    (
        rate_ref, slope_ref, sums_ref, dsums_ref, y_ref, dy_ref, adj_ref, dadj_ref, norm_ref, grad_ref, curve_ref,
    ) = refs
    rows = states * 4
    me = me_ref[0]
    unpack(piece_refs, wide_ref, me, each * rows)
    blocks = states * 4 // ROWS
    decay = states / (states - 1.0)
    branches = length_ref.shape[1]
    length = length_ref[...]
    toward = toward_ref[...]
    grow = jnp.exp(decay * length)
    pad = LANES - branches

    def column(row):
        wide = jnp.concatenate([row, jnp.zeros((1, pad), F32)], axis=1)
        return jnp.transpose(jnp.broadcast_to(wide, (LANES, LANES)))

    rate_ref[...] = column((grow - 1.0) / states)
    slope_ref[...] = column(decay * toward * grow / states)
    unused = jnp.zeros((grad_ref.shape[0] - branches * ROWS, LANES), F32)
    grad_ref[branches * ROWS :, :] = unused
    curve_ref[branches * ROWS :, :] = unused
    raw = weight_ref[...].astype(F32)
    quarter = [raw[:, part * LANES : (part + 1) * LANES] for part in range(4)]
    weight = jnp.concatenate(quarter + quarter, axis=0)

    offsets = [0]
    size = tips
    while size > 1:
        offsets.append(offsets[-1] + size)
        size //= 2

    def row(ref, at):
        return jnp.broadcast_to(ref[pl.ds(at, 1), :], (ROWS, LANES))

    def leaf(slot):
        tip = order_ref[slot]
        first = ((tip // each) ^ me) * (each * rows) + tip % each
        x = wide_ref[pl.ds(first, rows, each), :].reshape(blocks, ROWS, LANES)
        total = both(part_sum(x))
        lift = row(rate_ref, tip) * total
        y = x + lift[None]
        y_ref[slot] = y
        sums_ref[slot] = total
        return y, row(slope_ref, tip) * total, total + states * lift

    def cherry(k):
        ya, qa, ta = leaf(2 * k)
        yb, qb, tb = leaf(2 * k + 1)
        z = ya * yb
        dz = qa[None] * yb + qb[None] * ya
        return z, dz, both(part_sum(z)), qa * tb + qb * ta

    def inner(at, z, dz, total, dtotal):
        rate, slope = row(rate_ref, at), row(slope_ref, at)
        y = z + (rate * total)[None]
        dy = dz + (rate * dtotal + slope * total)[None]
        y_ref[at] = y
        dy_ref[at - tips] = dy
        sums_ref[at] = total
        dsums_ref[at - tips] = dtotal
        return y, dy

    def join(left, right):
        (ya, dya), (yb, dyb) = left, right
        z = ya * yb
        dz = dya * yb + ya * dyb
        return z, dz, both(part_sum(z)), both(part_sum(dz))

    def climb(level, k, low):
        if level == 1:
            return cherry(k)
        kids = []
        for child in (2 * k, 2 * k + 1):
            kids.append(inner(offsets[level - 1] + child, *climb(level - 1, child, low)))
        return join(*kids)

    levels = len(offsets) - 1
    cut = 3

    def up(k, carry):
        z, dz, total, dtotal = climb(cut, k, 0)
        scale = states / total
        norm_ref[k] = scale
        inner(offsets[cut] + k, z * scale[None], dz * scale[None], jnp.full_like(total, states), dtotal * scale)
        return carry

    lax.fori_loop(0, tips >> cut, up, 0)

    def fetch(at):
        return y_ref[at], dy_ref[at - tips]

    def climb_top(level, k):
        if level == cut:
            return fetch(offsets[cut] + k)
        kids = [climb_top(level - 1, 2 * k), climb_top(level - 1, 2 * k + 1)]
        raw_values = join(*kids)
        if level == levels:
            return raw_values
        return inner(offsets[level] + k, *raw_values)

    _, _, total, dtotal = climb_top(levels, 0)
    seed = 1.0 / total
    dseed = -(dtotal * seed) * seed

    def record(row_at, total, dtotal, half, dhalf):
        share = row(rate_ref, row_at) + 1.0 / states
        both_totals = total * half
        here = pl.ds(pl.multiple_of(row_at * ROWS, ROWS), ROWS)
        grad_ref[here, :] = weight * (share * both_totals - 0.5)
        change = total * dhalf if dtotal is None else dtotal * half + total * dhalf
        curve_ref[here, :] = weight * (share * change + row(slope_ref, row_at) * both_totals)

    def down(at, ybar, dybar):
        half, dhalf = part_sum(ybar), part_sum(dybar)
        total, dtotal = sums_ref[at], dsums_ref[at - tips]
        record(at, total, dtotal, half, dhalf)
        full, dfull = both(half), both(dhalf)
        rate, slope = row(rate_ref, at), row(slope_ref, at)
        xbar = ybar + (rate * full)[None]
        dxbar = dybar + (rate * dfull + slope * full)[None]
        return xbar, dxbar, full * (1.0 + states * rate)

    def split(level, k, zbar, dzbar, zsum, low, emit):
        first, second = 2 * k, 2 * k + 1
        for child, other in ((first, second), (second, first)):
            if level == 1:
                yb = y_ref[other]
                half, dhalf = part_sum(zbar * yb), part_sum(dzbar * yb)
                tip, mate = order_ref[child], order_ref[other]
                total = sums_ref[child]
                push = row(slope_ref, mate) * sums_ref[other]
                record(tip, total, None, half, dhalf + 0.5 * (push * zsum))
                continue
            at, mate = offsets[level - 1] + child, offsets[level - 1] + other
            yb, dyb = fetch(mate)
            xbar, dxbar, xsum = down(at, zbar * yb, dzbar * yb + zbar * dyb)
            if level - 1 == low:
                emit(child, xbar, dxbar)
            else:
                split(level - 1, child, xbar, dxbar, xsum, low, emit)

    def keep(k, xbar, dxbar):
        scale = norm_ref[k][None]
        adj_ref[k] = xbar * scale
        dadj_ref[k] = dxbar * scale

    wide = (blocks, ROWS, LANES)
    split(levels, 0, jnp.broadcast_to(seed[None], wide), jnp.broadcast_to(dseed[None], wide), None, cut, keep)

    def descend(k, carry):
        split(cut, k, adj_ref[k], dadj_ref[k], None, 0, None)
        return carry

    lax.fori_loop(0, tips >> cut, descend, 0)

    def over_sites(ref):
        rows = part_sum([ref[pl.ds(part, LANES, ROWS), :] for part in range(ROWS)])
        return jnp.sum(jnp.transpose(rows), axis=0, keepdims=True)[:, :branches] * decay

    grad, curve = over_sites(grad_ref), over_sites(curve_ref)
    out_ref[...] = jnp.zeros_like(out_ref)
    out_ref[0:1, :branches] = grad
    out_ref[1:2, :branches] = curve
    out_ref[2:3, :] = jnp.broadcast_to(jnp.sum(0.5 * weight), (1, LANES))


def prune(pieces, me, unpack, leaf_order, site_weights, branch_length, direction, states, each):
    tips = leaf_order.shape[0]
    blocks = states * 4 // ROWS
    branches = branch_length.shape[0]
    tops = branches - tips
    cut = tips >> 3
    vm = pl.BlockSpec(memory_space=pltpu.VMEM)
    sm = pl.BlockSpec(memory_space=pltpu.SMEM)
    vec = (blocks, ROWS, LANES)
    return pl.pallas_call(
        functools.partial(
            prune_kernel, unpack=unpack, held=len(pieces), tips=tips, states=states, each=each
        ),
        in_specs=[sm, sm] + [vm] * (3 + len(pieces)),
        out_specs=vm,
        out_shape=jax.ShapeDtypeStruct((ROWS, LANES), F32),
        scratch_shapes=[
            pltpu.VMEM((tips * states * 4, LANES), F32),
            pltpu.VMEM((LANES, LANES), F32),
            pltpu.VMEM((LANES, LANES), F32),
            pltpu.VMEM((branches, ROWS, LANES), F32),
            pltpu.VMEM((tops, ROWS, LANES), F32),
            pltpu.VMEM((branches, *vec), F32),
            pltpu.VMEM((tops, *vec), F32),
            pltpu.VMEM((cut, *vec), F32),
            pltpu.VMEM((cut, *vec), F32),
            pltpu.VMEM((cut, ROWS, LANES), F32),
            pltpu.VMEM((LANES * ROWS, LANES), F32),
            pltpu.VMEM((LANES * ROWS, LANES), F32),
        ],
        compiler_params=pltpu.CompilerParams(vmem_limit_bytes=32 * 1024 * 1024),
        name="prune",
    )(
        leaf_order,
        me.reshape(1),
        site_weights.reshape(1, -1),
        branch_length.reshape(1, -1),
        direction.reshape(1, -1),
        *pieces,
    )


def unpack_plain(piece_refs, wide_ref, me, rows):
    (pieces,) = piece_refs
    for number in range(pieces.shape[0]):
        wide_ref[number * rows : (number + 1) * rows, :] = pieces[number].astype(F32)


def unpack_pairs(piece_refs, wide_ref, me, rows, early, late):
    own, first, *refs = piece_refs
    deep = own.shape[1]
    here = pl.ds(pl.multiple_of(lax.rem(me, 2) * deep, deep), deep)

    def put(number, block):
        wide_ref[number * rows : (number + 1) * rows, :] = block.astype(F32).reshape(rows, LANES)

    put(0, own[...])
    put(1, first[0])
    both_refs, late_refs, swapped_refs = refs[: len(early)], refs[len(early) :][: len(late)], refs[len(early) + len(late) :]
    for apart, block in zip(early, both_refs):
        put(2 * apart, block[:, here, :])
    for apart, block in zip(late, late_refs):
        put(2 * apart, block[0])
        put(2 * apart + 1, block[1])
    for number, apart in enumerate(early):
        block = swapped_refs[number // 2]
        put(2 * apart + 1, block[number % 2])


def by_tile(tip_probs):
    tips, states, sites = tip_probs.shape
    tiles = sites // LANES
    shaped = tip_probs.transpose(1, 0, 2).reshape(states, tips, tiles, LANES)
    return shaped.transpose(0, 2, 1, 3).reshape(states, tiles * tips, LANES)


def exchange_plain(probs):
    peers = lax.axis_size("sites")
    states, rows, _ = probs.shape
    blocks = probs.reshape(states, peers, rows // peers, LANES).transpose(1, 0, 2, 3)
    arrived = lax.all_to_all(blocks, "sites", 0, 0, tiled=True)
    return [arrived.reshape(peers, -1, LANES)], unpack_plain


def cut_kernel(me_ref, probs_ref, after_ref, *refs, firsts):
    out_refs, sems = refs[:-1], refs[-1]
    me = me_ref[0]
    copies = []
    for out_ref, places in zip(out_refs, firsts):
        for slot, first in enumerate(places):
            count = out_ref.shape[2]
            start = pl.multiple_of(first(me), count)
            source = probs_ref.at[:, pl.ds(start, count), :]
            copies.append(pltpu.make_async_copy(source, out_ref.at[slot], sems.at[len(copies)]))
    for copy in copies:
        copy.start()
    for copy in copies:
        copy.wait()


def cut(probs, me, firsts, counts, after):
    vm = pl.BlockSpec(memory_space=pltpu.VMEM)
    states = probs.shape[0]
    return pl.pallas_call(
        functools.partial(cut_kernel, firsts=firsts),
        in_specs=[
            pl.BlockSpec(memory_space=pltpu.SMEM),
            pl.BlockSpec(memory_space=pltpu.HBM),
            pl.BlockSpec(memory_space=pl.ANY),
        ],
        out_specs=[vm] * len(counts),
        out_shape=[
            jax.ShapeDtypeStruct((len(places), states, count, LANES), probs.dtype)
            for places, count in zip(firsts, counts)
        ],
        scratch_shapes=[pltpu.SemaphoreType.DMA((sum(len(places) for places in firsts),))],
        compiler_params=pltpu.CompilerParams(vmem_limit_bytes=16 * 1024 * 1024),
        name="cut",
    )(me.reshape(1), pltpu.with_memory_space_constraint(probs, pltpu.HBM), after)


def exchange_pairs(probs, me):
    peers = lax.axis_size("sites")
    chips = peers // 2
    core = me % 2
    states, rows, _ = probs.shape
    deep = rows // peers
    far, near = range(chips // 2, chips), [*range(2, chips // 2), 1]
    order = [far[0], *(apart for pair in zip(near, far[1:]) for apart in pair)]
    early, late = order[:-1], order[-1:]

    def chip_first(apart):
        return lambda me: ((me // 2) ^ apart) * (2 * deep)

    def core_first(step):
        return lambda me: (me ^ step) * deep

    firsts = [[chip_first(apart)] for apart in early]
    counts = [2 * deep] * len(early)
    head = cut(probs, me, firsts[:1], counts[:1], me.reshape(1))
    firsts += [[core_first(1), *(core_first(2 * apart + 1) for apart in late)]]
    firsts += [[core_first(2 * apart)] for apart in late]
    firsts += [[core_first(0)]]
    counts += [deep] * (len(late) + 2)
    tail = cut(probs, me, firsts[1:], counts[1:], head[0])
    sent = [*head, *tail[: len(early) - 1]]
    give, *mine, own = tail[len(early) - 1 :]

    def swap(block, step):
        return lax.ppermute(block, "sites", [(i, i ^ step) for i in range(peers)])

    first = swap(give, 1)
    got = [swap(block[0], 2 * apart) for apart, block in zip(early, sent)]
    for number, apart in enumerate(late):
        got.append(swap(jnp.concatenate([mine[number], first[number + 1 : number + 2]], axis=0), 2 * apart))
    other = deep * (1 - core)
    give = [lax.dynamic_slice(block, (0, other, 0), (states, deep, LANES)) for block in got[: len(early)]]
    swapped = [swap(jnp.stack(give[at : at + 2]), 1) for at in range(0, len(give), 2)]
    return [own[0], first, *got, *swapped], functools.partial(unpack_pairs, early=early, late=late)


def total_over_sites(part):
    peers = lax.axis_size("sites")
    steps, bit = [2, peers - 4], 4
    while bit < peers // 2:
        steps.append(bit)
        bit *= 2
    rounds = [[1]]
    for first in range(0, len(steps), 2):
        pair = steps[first : first + 2]
        rounds.append([step + 1 for step in ([*pair, pair[0] ^ pair[1]] if len(pair) > 1 else pair)])
    for apart in rounds:
        got = [lax.ppermute(part, "sites", [(i, i ^ step) for i in range(peers)]) for step in apart]
        part = part + got[0]
        if len(got) > 1:
            part = part + (got[1] + got[2])
    return part


def local(tip_probs, leaf_order, site_weights, branch_length, direction):
    branches = branch_length.shape[0]
    each, states, _ = tip_probs.shape
    probs = by_tile(tip_probs)
    if 4 * each % 16 == 0:
        me = lax.axis_index("sites").astype(jnp.int32)
        pieces, unpack = exchange_pairs(probs, me)
    else:
        me = jnp.zeros((), jnp.int32)
        pieces, unpack = exchange_plain(probs)
    part = prune(pieces, me, unpack, leaf_order, site_weights, branch_length, direction, states, each)
    sums = total_over_sites(part)[:, :branches]
    return sums[0] / sums[2], sums[1] / sums[2]


def solution(mesh):
    return jax.shard_map(
        local,
        mesh=mesh,
        in_specs=(
            P(("groups", "sites"), None, None),
            P("groups"),
            P(("groups", "sites")),
            P("groups"),
            P("groups"),
        ),
        out_specs=(P("groups"), P("groups")),
        check_vma=False,
    )
```

```python
import functools
import jax
import jax.numpy as jnp
from jax import lax
from jax.experimental import pallas as pl
from jax.experimental.pallas import tpu as pltpu
from jax.sharding import PartitionSpec as P

F32 = jnp.float32
LANES = 128
ROWS = 8


def part_sum(x):
    parts = [x[i] for i in range(len(x))]
    while len(parts) > 1:
        parts = [sum(parts[i + 1 : i + 2], parts[i]) for i in range(0, len(parts), 2)]
    return parts[0]


def both(half):
    return half + pltpu.roll(half, half.shape[0] // 2, 0)


def prune_kernel(
    order_ref, me_ref, *refs, unpack, held, tips, states, each
):
    (weight_ref, length_ref, toward_ref), piece_refs = refs[:3], refs[3 : 3 + held]
    out_ref, wide_ref, *refs = refs[3 + held :]
    (
        rate_ref, slope_ref, hold_ref, turn_ref, sums_ref, dsums_ref, y_ref, dy_ref, adj_ref, dadj_ref, norm_ref, grad_ref, curve_ref,
    ) = refs
    rows = states * 4
    me = me_ref[0]
    unpack(piece_refs, wide_ref, me, each * rows)
    blocks = states * 4 // ROWS
    decay = states / (states - 1.0)
    branches = length_ref.shape[1]
    length = length_ref[...]
    toward = toward_ref[...]
    grow = jnp.exp(decay * length)
    pad = LANES - branches

    def column(row):
        wide = jnp.concatenate([row, jnp.zeros((1, pad), F32)], axis=1)
        return jnp.transpose(jnp.broadcast_to(wide, (LANES, LANES)))

    rate_ref[...] = column((grow - 1.0) / states)
    slope_ref[...] = column(decay * toward * grow / states)
    share = (grow - 1.0) / states + 1.0 / states
    hold_ref[...] = column(0.5 / share)
    turn_ref[...] = column(decay * toward)
    unused = jnp.zeros((grad_ref.shape[0] - branches * ROWS, LANES), F32)
    grad_ref[branches * ROWS :, :] = unused
    curve_ref[branches * ROWS :, :] = unused
    raw = weight_ref[...].astype(F32)
    quarter = [raw[:, part * LANES : (part + 1) * LANES] for part in range(4)]
    weight = jnp.concatenate(quarter + quarter, axis=0)

    offsets = [0]
    size = tips
    while size > 1:
        offsets.append(offsets[-1] + size)
        size //= 2

    def row(ref, at):
        return jnp.broadcast_to(ref[pl.ds(at, 1), :], (ROWS, LANES))

    def leaf(slot):
        tip = order_ref[slot]
        first = ((tip // each) ^ me) * (each * rows) + tip % each
        x = wide_ref[pl.ds(first, rows, each), :].reshape(blocks, ROWS, LANES)
        total = both(part_sum(x))
        lift = row(rate_ref, tip) * total
        y = x + lift[None]
        y_ref[slot] = y
        sums_ref[slot] = total
        return y, row(slope_ref, tip) * total, total + states * lift

    def cherry(k):
        ya, qa, ta = leaf(2 * k)
        yb, qb, tb = leaf(2 * k + 1)
        z = ya * yb
        dz = qa[None] * yb + qb[None] * ya
        return z, dz, both(part_sum(z)), qa * tb + qb * ta

    def inner(at, z, dz, total, dtotal):
        rate, slope = row(rate_ref, at), row(slope_ref, at)
        y = z + (rate * total)[None]
        dy = dz + (rate * dtotal + slope * total)[None]
        y_ref[at] = y
        dy_ref[at - tips] = dy
        sums_ref[at] = total
        dsums_ref[at - tips] = dtotal
        return y, dy

    def join(left, right):
        (ya, dya), (yb, dyb) = left, right
        z = ya * yb
        dz = dya * yb + ya * dyb
        return z, dz, both(part_sum(z)), both(part_sum(dz))

    def climb(level, k, low):
        if level == 1:
            return cherry(k)
        kids = []
        for child in (2 * k, 2 * k + 1):
            kids.append(inner(offsets[level - 1] + child, *climb(level - 1, child, low)))
        return join(*kids)

    levels = len(offsets) - 1
    cut = 3

    def up(k, carry):
        z, dz, total, dtotal = climb(cut, k, 0)
        scale = states / total
        norm_ref[k] = scale
        inner(offsets[cut] + k, z * scale[None], dz * scale[None], jnp.full_like(total, states), dtotal * scale)
        return carry

    lax.fori_loop(0, tips >> cut, up, 0)

    def fetch(at):
        return y_ref[at], dy_ref[at - tips]

    def climb_top(level, k):
        if level == cut:
            return fetch(offsets[cut] + k)
        kids = [climb_top(level - 1, 2 * k), climb_top(level - 1, 2 * k + 1)]
        raw_values = join(*kids)
        if level == levels:
            return raw_values
        return inner(offsets[level] + k, *raw_values)

    _, _, total, dtotal = climb_top(levels, 0)
    seed = 1.0 / total
    dseed = -(dtotal * seed) * seed

    def record(row_at, total, dtotal, half, dhalf):
        both_totals = total * half
        here = pl.ds(pl.multiple_of(row_at * ROWS, ROWS), ROWS)
        grad_ref[here, :] = weight * (both_totals - row(hold_ref, row_at))
        change = total * dhalf if dtotal is None else dtotal * half + total * dhalf
        curve_ref[here, :] = weight * (change + row(turn_ref, row_at) * both_totals)

    def down(at, ybar, dybar):
        half, dhalf = part_sum(ybar), part_sum(dybar)
        total, dtotal = sums_ref[at], dsums_ref[at - tips]
        record(at, total, dtotal, half, dhalf)
        full, dfull = both(half), both(dhalf)
        rate, slope = row(rate_ref, at), row(slope_ref, at)
        xbar = ybar + (rate * full)[None]
        dxbar = dybar + (rate * dfull + slope * full)[None]
        return xbar, dxbar, full * (1.0 + states * rate)

    def split(level, k, zbar, dzbar, zsum, low, emit):
        first, second = 2 * k, 2 * k + 1
        for child, other in ((first, second), (second, first)):
            if level == 1:
                yb = y_ref[other]
                half, dhalf = part_sum(zbar * yb), part_sum(dzbar * yb)
                tip, mate = order_ref[child], order_ref[other]
                total = sums_ref[child]
                push = row(slope_ref, mate) * sums_ref[other]
                record(tip, total, None, half, dhalf + 0.5 * (push * zsum))
                continue
            at, mate = offsets[level - 1] + child, offsets[level - 1] + other
            yb, dyb = fetch(mate)
            xbar, dxbar, xsum = down(at, zbar * yb, dzbar * yb + zbar * dyb)
            if level - 1 == low:
                emit(child, xbar, dxbar)
            else:
                split(level - 1, child, xbar, dxbar, xsum, low, emit)

    def keep(k, xbar, dxbar):
        scale = norm_ref[k][None]
        adj_ref[k] = xbar * scale
        dadj_ref[k] = dxbar * scale

    wide = (blocks, ROWS, LANES)
    split(levels, 0, jnp.broadcast_to(seed[None], wide), jnp.broadcast_to(dseed[None], wide), None, cut, keep)

    def descend(k, carry):
        split(cut, k, adj_ref[k], dadj_ref[k], None, 0, None)
        return carry

    lax.fori_loop(0, tips >> cut, descend, 0)

    def over_sites(ref):
        rows = part_sum([ref[pl.ds(part, LANES, ROWS), :] for part in range(ROWS)])
        return jnp.sum(jnp.transpose(rows), axis=0, keepdims=True)[:, :branches] * (decay * share)

    grad, curve = over_sites(grad_ref), over_sites(curve_ref)
    out_ref[...] = jnp.zeros_like(out_ref)
    out_ref[0:1, :branches] = grad
    out_ref[1:2, :branches] = curve
    out_ref[2:3, :] = jnp.broadcast_to(jnp.sum(0.5 * weight), (1, LANES))


def prune(pieces, me, unpack, leaf_order, site_weights, branch_length, direction, states, each):
    tips = leaf_order.shape[0]
    blocks = states * 4 // ROWS
    branches = branch_length.shape[0]
    tops = branches - tips
    cut = tips >> 3
    vm = pl.BlockSpec(memory_space=pltpu.VMEM)
    sm = pl.BlockSpec(memory_space=pltpu.SMEM)
    vec = (blocks, ROWS, LANES)
    return pl.pallas_call(
        functools.partial(
            prune_kernel, unpack=unpack, held=len(pieces), tips=tips, states=states, each=each
        ),
        in_specs=[sm, sm] + [vm] * (3 + len(pieces)),
        out_specs=vm,
        out_shape=jax.ShapeDtypeStruct((ROWS, LANES), F32),
        scratch_shapes=[
            pltpu.VMEM((tips * states * 4, LANES), F32),
            pltpu.VMEM((LANES, LANES), F32),
            pltpu.VMEM((LANES, LANES), F32),
            pltpu.VMEM((LANES, LANES), F32),
            pltpu.VMEM((LANES, LANES), F32),
            pltpu.VMEM((branches, ROWS, LANES), F32),
            pltpu.VMEM((tops, ROWS, LANES), F32),
            pltpu.VMEM((branches, *vec), F32),
            pltpu.VMEM((tops, *vec), F32),
            pltpu.VMEM((cut, *vec), F32),
            pltpu.VMEM((cut, *vec), F32),
            pltpu.VMEM((cut, ROWS, LANES), F32),
            pltpu.VMEM((LANES * ROWS, LANES), F32),
            pltpu.VMEM((LANES * ROWS, LANES), F32),
        ],
        compiler_params=pltpu.CompilerParams(vmem_limit_bytes=32 * 1024 * 1024),
        name="prune",
    )(
        leaf_order,
        me.reshape(1),
        site_weights.reshape(1, -1),
        branch_length.reshape(1, -1),
        direction.reshape(1, -1),
        *pieces,
    )


def unpack_plain(piece_refs, wide_ref, me, rows):
    (pieces,) = piece_refs
    for number in range(pieces.shape[0]):
        wide_ref[number * rows : (number + 1) * rows, :] = pieces[number].astype(F32)


def unpack_pairs(piece_refs, wide_ref, me, rows, early, late):
    own, first, *refs = piece_refs
    deep = own.shape[1]
    here = pl.ds(pl.multiple_of(lax.rem(me, 2) * deep, deep), deep)

    def put(number, block):
        wide_ref[number * rows : (number + 1) * rows, :] = block.astype(F32).reshape(rows, LANES)

    put(0, own[...])
    put(1, first[0])
    both_refs, late_refs, swapped_refs = refs[: len(early)], refs[len(early) :][: len(late)], refs[len(early) + len(late) :]
    for apart, block in zip(early, both_refs):
        put(2 * apart, block[:, here, :])
    for apart, block in zip(late, late_refs):
        put(2 * apart, block[0])
        put(2 * apart + 1, block[1])
    for number, apart in enumerate(early):
        block = swapped_refs[number // 2]
        put(2 * apart + 1, block[number % 2])


def by_tile(tip_probs):
    tips, states, sites = tip_probs.shape
    tiles = sites // LANES
    shaped = tip_probs.transpose(1, 0, 2).reshape(states, tips, tiles, LANES)
    return shaped.transpose(0, 2, 1, 3).reshape(states, tiles * tips, LANES)


def exchange_plain(probs):
    peers = lax.axis_size("sites")
    states, rows, _ = probs.shape
    blocks = probs.reshape(states, peers, rows // peers, LANES).transpose(1, 0, 2, 3)
    arrived = lax.all_to_all(blocks, "sites", 0, 0, tiled=True)
    return [arrived.reshape(peers, -1, LANES)], unpack_plain


def cut_kernel(me_ref, probs_ref, after_ref, *refs, firsts):
    out_refs, sems = refs[:-1], refs[-1]
    me = me_ref[0]
    copies = []
    for out_ref, places in zip(out_refs, firsts):
        for slot, first in enumerate(places):
            count = out_ref.shape[2]
            start = pl.multiple_of(first(me), count)
            source = probs_ref.at[:, pl.ds(start, count), :]
            copies.append(pltpu.make_async_copy(source, out_ref.at[slot], sems.at[len(copies)]))
    for copy in copies:
        copy.start()
    for copy in copies:
        copy.wait()


def cut(probs, me, firsts, counts, after):
    vm = pl.BlockSpec(memory_space=pltpu.VMEM)
    states = probs.shape[0]
    return pl.pallas_call(
        functools.partial(cut_kernel, firsts=firsts),
        in_specs=[
            pl.BlockSpec(memory_space=pltpu.SMEM),
            pl.BlockSpec(memory_space=pltpu.HBM),
            pl.BlockSpec(memory_space=pl.ANY),
        ],
        out_specs=[vm] * len(counts),
        out_shape=[
            jax.ShapeDtypeStruct((len(places), states, count, LANES), probs.dtype)
            for places, count in zip(firsts, counts)
        ],
        scratch_shapes=[pltpu.SemaphoreType.DMA((sum(len(places) for places in firsts),))],
        compiler_params=pltpu.CompilerParams(vmem_limit_bytes=16 * 1024 * 1024),
        name="cut",
    )(me.reshape(1), pltpu.with_memory_space_constraint(probs, pltpu.HBM), after)


def exchange_pairs(probs, me):
    peers = lax.axis_size("sites")
    chips = peers // 2
    core = me % 2
    states, rows, _ = probs.shape
    deep = rows // peers
    far, near = range(chips // 2, chips), [*range(2, chips // 2), 1]
    order = [far[0], *(apart for pair in zip(near, far[1:]) for apart in pair)]
    early, late = order[:-1], order[-1:]

    def chip_first(apart):
        return lambda me: ((me // 2) ^ apart) * (2 * deep)

    def core_first(step):
        return lambda me: (me ^ step) * deep

    firsts = [[chip_first(apart)] for apart in early]
    counts = [2 * deep] * len(early)
    head = cut(probs, me, firsts[:1], counts[:1], me.reshape(1))
    firsts += [[core_first(1), *(core_first(2 * apart + 1) for apart in late)]]
    firsts += [[core_first(2 * apart)] for apart in late]
    firsts += [[core_first(0)]]
    counts += [deep] * (len(late) + 2)
    tail = cut(probs, me, firsts[1:], counts[1:], head[0])
    sent = [*head, *tail[: len(early) - 1]]
    give, *mine, own = tail[len(early) - 1 :]

    def swap(block, step):
        return lax.ppermute(block, "sites", [(i, i ^ step) for i in range(peers)])

    first = swap(give, 1)
    got = [swap(block[0], 2 * apart) for apart, block in zip(early, sent)]
    for number, apart in enumerate(late):
        got.append(swap(jnp.concatenate([mine[number], first[number + 1 : number + 2]], axis=0), 2 * apart))
    other = deep * (1 - core)
    give = [lax.dynamic_slice(block, (0, other, 0), (states, deep, LANES)) for block in got[: len(early)]]
    swapped = [swap(jnp.stack(give[at : at + 2]), 1) for at in range(0, len(give), 2)]
    return [own[0], first, *got, *swapped], functools.partial(unpack_pairs, early=early, late=late)


def total_over_sites(part):
    peers = lax.axis_size("sites")
    steps, bit = [2, peers - 4], 4
    while bit < peers // 2:
        steps.append(bit)
        bit *= 2
    rounds = [[1]]
    for first in range(0, len(steps), 2):
        pair = steps[first : first + 2]
        rounds.append([step + 1 for step in ([*pair, pair[0] ^ pair[1]] if len(pair) > 1 else pair)])
    for apart in rounds:
        got = [lax.ppermute(part, "sites", [(i, i ^ step) for i in range(peers)]) for step in apart]
        part = part + got[0]
        if len(got) > 1:
            part = part + (got[1] + got[2])
    return part


def local(tip_probs, leaf_order, site_weights, branch_length, direction):
    branches = branch_length.shape[0]
    each, states, _ = tip_probs.shape
    probs = by_tile(tip_probs)
    if 4 * each % 16 == 0:
        me = lax.axis_index("sites").astype(jnp.int32)
        pieces, unpack = exchange_pairs(probs, me)
    else:
        me = jnp.zeros((), jnp.int32)
        pieces, unpack = exchange_plain(probs)
    part = prune(pieces, me, unpack, leaf_order, site_weights, branch_length, direction, states, each)
    sums = total_over_sites(part)[:, :branches]
    return sums[0] / sums[2], sums[1] / sums[2]


def solution(mesh):
    return jax.shard_map(
        local,
        mesh=mesh,
        in_specs=(
            P(("groups", "sites"), None, None),
            P("groups"),
            P(("groups", "sites")),
            P("groups"),
            P("groups"),
        ),
        out_specs=(P("groups"), P("groups")),
        check_vma=False,
    )
```
